128 devices in a mesh: row: 16 (over y_lo, z, core), col: 8 (over x, y_hi).
Axes of the slice: x: 4, y: 4 (y_hi: 2, y_lo: 2; y = y_hi * 2 + y_lo), z: 4, core: 2. Of those that a mesh axis runs over, the one named last changes fastest.
Arguments:
- tokens: bfloat16 [2048, 8192], P('row', 'col'), may hold values from -6 to 6
- gate_weight: bfloat16 [8192, 14336], P('col', 'row'), may hold values from -0.109375 to 0.109375
- up_weight: bfloat16 [8192, 14336], P('col', 'row'), may hold values from -0.109375 to 0.109375
- down_weight: bfloat16 [14336, 8192], P('row', 'col'), may hold values from -0.09375 to 0.09375
- input_mask: int32 [64, 112], P('col', 'row'), may hold values from 0 to 1, as said below
- output_mask: int32 [112, 64], P('row', 'col'), may hold values from 0 to 1, as said below
- cotangent: bfloat16 [2048, 8192], P('row', 'col'), may hold values from -6 to 6
Outputs:
- output: bfloat16 [2048, 8192], P('row', 'col')
- grad_gate: float32 [8192, 14336], P('col', 'row')
- grad_up: float32 [8192, 14336], P('col', 'row')
- grad_down: float32 [14336, 8192], P('row', 'col')
The draws below stay inside these ranges and needn't reach their ends.
Inputs may be any that keep to these rules, and one draw needn't show every extreme that they name: `input_mask`: entries are 0 or 1; some 30 percent are 1, a share that differs from one column of blocks to another. `output_mask`: entries are 0 or 1; some 30 percent are 1, a share that differs from one row of blocks to another.
All inputs are finite; a program needn't handle non-finite values.
Results may differ from the reference program's by a relative error of at most 0.0049.
Values may be sent and summed in bfloat16 or wider, within the bound.
A program may use at most 192 MiB of HBM per device.

```python
import jax
import jax.numpy as jnp

D = 8192
FF = 14336
BLK = 128
TOKENS = 2048


def keep_table(key, rows, cols, rate_shape):
    rate = jax.random.randint(jax.random.fold_in(key, 1), rate_shape, 50, 550)
    roll = jax.random.randint(jax.random.fold_in(key, 2), (rows, cols), 0, 1000)
    return (roll < rate).astype(jnp.int32)


def draw_input_mask(key, part):
    key = jax.random.fold_in(key, 11)
    return keep_table(key, D // BLK, FF // BLK, (1, FF // BLK))


def draw_output_mask(key, part):
    key = jax.random.fold_in(key, 12)
    return keep_table(key, FF // BLK, D // BLK, (FF // BLK, 1))


def level_of(key, dims, cuts, low, high):
    loudness = 1.0
    for axis_at, shards_of in cuts:
        steps = jax.random.uniform(jax.random.fold_in(jax.random.fold_in(key, 6), axis_at), (shards_of,), jnp.float32, low / len(cuts), high / len(cuts))
        loudness = loudness * jnp.repeat(jnp.exp(steps), dims[axis_at] // shards_of).reshape((-1,) + (1,) * (len(dims) - 1 - axis_at))
    return loudness


def centred(own_key, shape, spread, bound, pieces=(), held_as=jnp.bfloat16):
    loudness = level_of(own_key, shape, pieces, -0.22, 0.18) if pieces else 1.0
    drawn = jax.random.normal(own_key, shape, jnp.float32) * spread * loudness
    return jnp.minimum(jnp.maximum(drawn, -bound), bound).astype(held_as)


def setup_inputs(seed: int = 0) -> dict:
    key_of = jax.random.split(jax.random.key(seed), 8)
    tokens = centred(key_of[0], (TOKENS, D), 1.0, 6.0, ((0, 16), (1, 8)))
    gate_weight = centred(key_of[1], (D, FF), (D // 3) ** -0.5, 0.109375, ((0, 8), (1, 16)))
    up_weight = centred(key_of[2], (D, FF), (D // 3) ** -0.5, 0.109375, ((0, 8), (1, 16)))
    down_weight = centred(key_of[3], (FF, D), (FF // 3) ** -0.5, 0.09375, ((0, 16), (1, 8)))
    input_mask = draw_input_mask(jax.random.fold_in(key_of[7], 71), 0)
    output_mask = draw_output_mask(jax.random.fold_in(key_of[7], 71), 0)
    cotangent = centred(key_of[6], (TOKENS, D), 1.0, 6.0, ((0, 16), (1, 8)))
    return dict(tokens=tokens, gate_weight=gate_weight, up_weight=up_weight, down_weight=down_weight, input_mask=input_mask, output_mask=output_mask, cotangent=cotangent)


def expand(mask):
    return jnp.repeat(jnp.repeat(mask, BLK, axis=0), BLK, axis=1) > 0


def reference(tokens, gate_weight, up_weight, down_weight, input_mask, output_mask, cotangent):
    keep_in = expand(input_mask)
    keep_out = expand(output_mask)
    nothing = jnp.zeros((), jnp.bfloat16)
    gate_kept = jnp.where(keep_in, gate_weight, nothing)
    up_kept = jnp.where(keep_in, up_weight, nothing)
    down_kept = jnp.where(keep_out, down_weight, nothing)
    gate = jnp.dot(tokens, gate_kept, preferred_element_type=jnp.float32)
    upper = jnp.dot(tokens, up_kept, preferred_element_type=jnp.float32)
    sigma = jax.nn.sigmoid(gate)
    swish = gate * sigma
    hidden = (swish * upper).astype(jnp.bfloat16)
    output = jnp.dot(hidden, down_kept, preferred_element_type=jnp.float32).astype(jnp.bfloat16)
    grad_hidden = jnp.dot(cotangent, down_kept.T, preferred_element_type=jnp.float32)
    gate_pre = (grad_hidden * upper * sigma * (1.0 + gate * (1.0 - sigma))).astype(jnp.bfloat16)
    up_pre = (grad_hidden * swish).astype(jnp.bfloat16)
    zero = jnp.zeros((), jnp.float32)
    grad_down = jnp.where(keep_out, jnp.dot(hidden.T, cotangent, preferred_element_type=jnp.float32), zero)
    grad_gate = jnp.where(keep_in, jnp.dot(tokens.T, gate_pre, preferred_element_type=jnp.float32), zero)
    grad_up = jnp.where(keep_in, jnp.dot(tokens.T, up_pre, preferred_element_type=jnp.float32), zero)
    return output, grad_gate, grad_up, grad_down
```

```python
import jax
import jax.numpy as jnp
from jax import lax
from jax.experimental import pallas as pl
from jax.experimental.pallas import tpu as pltpu
from jax.sharding import PartitionSpec as P

BLK = 128
BF = jnp.bfloat16
F32 = jnp.float32
MESH = pl.DeviceIdType.MESH
VMEM_LIMIT = 62 * 2**20
SLOTS = 96


def aligned(start, size, to=128):
    return pl.ds(pl.multiple_of(start, to), size)


def forward_kernel(
    tok, cot, gate_w, up_w, down_w, keep_in, keep_out,
    out, tok_hbm, cot_hbm, hid_hbm, grd_hbm,
    w_in, w_down, tok_all, cot_all,
    u_s2, u_sp, u_sm, u_ia, u_ib, u_rp, u_rm, u_ys, u_yr, u_own,
    h_s2, h_sp, h_sm, h_ia, h_ib, h_rp, h_rm, h_ys, h_yr, h_own,
    hid_own, grd_own, hid_all,
    c_s, c_r, z_s2, z_i, z_sp, z_sm, z_rp, z_rm, o_ys, o_yr, o_own,
    send_sem, recv_sem, local_sem,
):
    row = lax.axis_index("row")
    col = lax.axis_index("col")
    x, h = col // 2, col % 2
    yl, z, c = row // 8, (row // 2) % 4, row % 2

    def device(x_, h_, yl_, z_, c_):
        return (yl_ * 8 + z_ * 2 + c_, x_ * 2 + h_)

    xp = device((x + 1) % 4, h, yl, z, c)
    xm = device((x + 3) % 4, h, yl, z, c)
    yh = device(x, 1 - h, yl, z, c)
    yn = device(x, h, 1 - yl, z, c)
    zp = device(x, h, yl, (z + 1) % 4, c)
    zm = device(x, h, yl, (z + 3) % 4, c)
    co = device(x, h, yl, z, 1 - c)
    peers = (xp, xm, yh, yn, zp, zm, co)

    slot = [0]
    sent = []

    def send(src, dst, peer):
        i = slot[0]
        slot[0] += 1
        copy = pltpu.make_async_remote_copy(
            src_ref=src, dst_ref=dst, send_sem=send_sem.at[i], recv_sem=recv_sem.at[i],
            device_id=peer, device_id_type=MESH,
        )
        copy.start()
        sent.append(copy)
        return copy

    locals_ = [0]

    def local(src, dst):
        copy = pltpu.make_async_copy(src, dst, local_sem.at[locals_[0]])
        locals_[0] += 1
        copy.start()
        return copy

    loads = [
        local(gate_w, w_in.at[:, 0:896]),
        local(up_w, w_in.at[:, 896:1792]),
        local(down_w, w_down),
    ]

    barrier = pltpu.get_barrier_semaphore()
    for peer in peers:
        pl.semaphore_signal(barrier, inc=1, device_id=peer, device_id_type=MESH)
    pl.semaphore_wait(barrier, len(peers))

    def block(yl_, z_, c_):
        return yl_ * 8 + z_ * 2 + c_

    def rows(b, part=0, size=128):
        return aligned(b * 128 + part * 64, size, 64)

    def gather_row(own, whole):
        me = block(yl, z, c)
        spot = whole.at[rows(me)]
        to_y = send(own, spot, yn)
        own_p, own_m = send(own, spot, zp), send(own, spot, zm)
        cores = [send(own, spot, co)]
        whole[rows(me), :] = own[...]
        yield
        to_y.wait_recv()
        spot = whole.at[rows(block(1 - yl, z, c))]
        mate_p, mate_m = send(spot, spot, zp), send(spot, spot, zm)
        cores.append(send(spot, spot, co))
        halves = []
        for y_, from_m, from_p in ((yl, own_p, own_m), (1 - yl, mate_p, mate_m)):
            from_m.wait_recv()
            b = block(y_, (z + 3) % 4, c)
            spot = whole.at[rows(b, 0, 64)]
            first = send(spot, spot, zp)
            spot = whole.at[rows(b)]
            cores.append(send(spot, spot, co))
            from_p.wait_recv()
            b = block(y_, (z + 1) % 4, c)
            spot = whole.at[rows(b, 1, 64)]
            second = send(spot, spot, zm)
            spot = whole.at[rows(b)]
            cores.append(send(spot, spot, co))
            halves.append((y_, first, second))
        yield
        for y_, first, second in halves:
            first.wait_recv()
            second.wait_recv()
            spot = whole.at[rows(block(y_, (z + 2) % 4, c))]
            cores.append(send(spot, spot, co))
        for copy in cores:
            copy.wait_recv()
        yield

    tok_steps = gather_row(tok, tok_all)
    cot_steps = gather_row(cot, cot_all)
    next(tok_steps)

    for copy in loads:
        copy.wait()
    for i in range(8):
        at = slice(i * 128, i * 128 + 128)
        for j in range(2):
            cols = slice(j * 896, j * 896 + 896)
            w_in[at, cols] = jnp.where(
                keep_in[i : i + 1, :] > 0, w_in[at, cols].astype(F32), 0.0
            ).astype(BF)
    for i in range(7):
        at = slice(i * 128, i * 128 + 128)
        w_down[at, :] = jnp.where(
            keep_out[i : i + 1, :] > 0, w_down[at, :].astype(F32), 0.0
        ).astype(BF)

    next(tok_steps)
    next(cot_steps)
    next(tok_steps)
    stores = [local(tok_all, tok_hbm)]

    def gate_up(chunk, half, emit):
        lhs = aligned(chunk * 512 + half * 256, 256, 256)

        @pl.loop(0, 7)
        def _(t):
            cols = aligned(t * 256, 256, 256)
            emit(jnp.dot(tok_all[lhs, :], w_in[:, cols], preferred_element_type=F32), cols)

    def grad_hidden(chunk, half, emit):
        lhs = aligned(chunk * 512 + half * 256, 256, 256)

        def tile(start, size):
            emit(
                lax.dot_general(
                    cot_all[lhs, :], w_down[aligned(start, size), :],
                    (((1,), (1,)), ((), ())), preferred_element_type=F32,
                ),
                aligned(start, size),
            )

        @pl.loop(0, 3)
        def _(t):
            tile(t * 256, 256)

        tile(768, 128)

    def put(buf, half):
        def emit(v, cols):
            buf[half * 256 : half * 256 + 256, cols] = v.astype(BF)
        return emit

    def put_sum(buf, half, inc):
        def emit(v, cols):
            buf[half * 256 : half * 256 + 256, cols] = (v + inc[:, cols].astype(F32)).astype(BF)
        return emit

    def reduce_col(product, s2, sp, sm, ia, ib, rp, rm, ys, yr, own):
        far, after, before = (x + 2) % 4, (x + 1) % 4, (x + 3) % 4
        lo, hi = slice(0, 256), slice(256, 512)
        product(far, 0, put(s2, 0))
        mid_a = send(s2.at[lo], ia, xp)
        product(far, 1, put(s2, 1))
        mid_b = send(s2.at[hi], ib, xm)
        product(after, 1, put(sp, 1))
        fin = [send(sp.at[hi], rp.at[hi], xp)]
        product(before, 0, put(sm, 0))
        fin.append(send(sm.at[lo], rm.at[lo], xm))
        yield
        mid_a.wait_recv()
        product(after, 0, put_sum(sp, 0, ia))
        fin.append(send(sp.at[lo], rp.at[lo], xp))
        mid_b.wait_recv()
        product(before, 1, put_sum(sm, 1, ib))
        fin.append(send(sm.at[hi], rm.at[hi], xm))
        yield
        for copy in fin:
            copy.wait_recv()

        def emit_total(half, target):
            at = aligned(half * 256, 256, 256)

            def emit(v, cols):
                total = v + rp[at, cols].astype(F32) + rm[at, cols].astype(F32)
                target[:, cols] = total.astype(target.dtype)
            return emit

        product(x, 1 - h, emit_total(1 - h, ys))
        over = send(ys, yr, yh)
        product(x, h, emit_total(h, own))
        yield
        over.wait_recv()
        yield

    def gather_col(own, whole):
        def spot_of(x_, h_, part=0, size=256):
            return whole.at[aligned(x_ * 512 + h_ * 256 + part * 128, size)]

        spot = spot_of(x, h)
        to_y = send(own, spot, yh)
        own_p, own_m = send(own, spot, xp), send(own, spot, xm)
        mine = local(own, spot)
        yield
        to_y.wait_recv()
        spot = spot_of(x, 1 - h)
        mate_p, mate_m = send(spot, spot, xp), send(spot, spot, xm)
        yield
        halves = []
        for h_, from_m, from_p in ((h, own_p, own_m), (1 - h, mate_p, mate_m)):
            from_m.wait_recv()
            spot = spot_of((x + 3) % 4, h_, 0, 128)
            halves.append(send(spot, spot, xp))
            from_p.wait_recv()
            spot = spot_of((x + 1) % 4, h_, 1, 128)
            halves.append(send(spot, spot, xm))
            yield
        for copy in halves:
            copy.wait_recv()
        mine.wait()
        yield

    up_steps = reduce_col(gate_up, u_s2, u_sp, u_sm, u_ia, u_ib, u_rp, u_rm, u_ys, u_yr, u_own)
    gh_steps = reduce_col(grad_hidden, h_s2, h_sp, h_sm, h_ia, h_ib, h_rp, h_rm, h_ys, h_yr, h_own)
    next(up_steps)
    next(cot_steps)
    next(cot_steps)
    stores.append(local(cot_all, cot_hbm))
    next(up_steps)
    next(gh_steps)
    next(up_steps)
    next(gh_steps)
    next(up_steps)

    @pl.loop(0, 16)
    def _(t):
        at = aligned(t * 16, 16, 16)
        gate = u_own[at, 0:896] + u_yr[at, 0:896].astype(F32)
        upper = u_own[at, 896:1792] + u_yr[at, 896:1792].astype(F32)
        sigma = 1.0 / (1.0 + jnp.exp(-gate))
        swish = gate * sigma
        hid_own[at, :] = (swish * upper).astype(BF)
        u_own[at, 0:896] = upper * sigma * (1.0 + gate * (1.0 - sigma))
        u_own[at, 896:1792] = swish

    hid_steps = gather_col(hid_own, hid_all)
    next(hid_steps)
    next(gh_steps)
    next(hid_steps)
    next(hid_steps)
    next(gh_steps)

    @pl.loop(0, 16)
    def _(t):
        at = aligned(t * 16, 16, 16)
        grad = h_own[at, :] + h_yr[at, :].astype(F32)
        grd_own[at, 0:896] = (grad * u_own[at, 0:896]).astype(BF)
        grd_own[at, 896:1792] = (grad * u_own[at, 896:1792]).astype(BF)

    grd_steps = gather_col(grd_own, grd_hbm)
    next(grd_steps)
    next(hid_steps)
    next(hid_steps)
    stores.append(local(hid_all, hid_hbm))

    def output_of(b):
        return jnp.dot(hid_all[rows(b), :], w_down[...], preferred_element_type=F32)

    def kept(yl_, z_):
        def piece(cols):
            part = jnp.dot(
                hid_all[rows(block(yl_, z_, c)), :], w_down[:, cols], preferred_element_type=F32
            )
            return part + c_r[yl_ * 4 + z_, :, cols]
        return piece

    def over_cols(body):
        @pl.loop(0, 4)
        def _(t):
            body(aligned(t * 256, 256, 256))

    for y_ in range(2):
        @pl.loop(0, 4)
        def _(z_):
            def body(cols):
                c_s[y_ * 4 + z_, :, cols] = jnp.dot(
                    hid_all[rows(block(y_, z_, 1 - c)), :], w_down[:, cols],
                    preferred_element_type=F32,
                )
            over_cols(body)

        if y_ == 0:
            core_0 = send(c_s.at[0:4], c_r.at[0:4], co)
        else:
            core_1 = send(c_s.at[4:8], c_r.at[4:8], co)

    next(grd_steps)
    core_0.wait_recv()
    core_1.wait_recv()
    far, after, before = (z + 2) % 4, (z + 1) % 4, (z + 3) % 4

    def ring_piece(y_, z_, target, inc=None):
        piece = kept(y_, z_)

        def body(cols):
            v = piece(cols)
            if inc is not None:
                v = v + inc[:, cols]
            target[:, cols] = v
        over_cols(body)

    ring_piece(0, far, z_s2.at[0])
    z_mid_a = send(z_s2.at[0], z_i.at[0], zp)
    ring_piece(1, far, z_s2.at[1])
    z_mid_b = send(z_s2.at[1], z_i.at[1], zm)
    ring_piece(1, after, z_sp.at[1])
    z_fin = [send(z_sp.at[1], z_rp.at[1], zp)]
    ring_piece(0, before, z_sm.at[0])
    z_fin.append(send(z_sm.at[0], z_rm.at[0], zm))
    next(grd_steps)
    z_mid_a.wait_recv()
    ring_piece(0, after, z_sp.at[0], z_i.at[0])
    z_fin.append(send(z_sp.at[0], z_rp.at[0], zp))
    z_mid_b.wait_recv()
    ring_piece(1, before, z_sm.at[1], z_i.at[1])
    z_fin.append(send(z_sm.at[1], z_rm.at[1], zm))
    next(grd_steps)
    for copy in z_fin:
        copy.wait_recv()

    def row_total(y_, target):
        piece = kept(y_, z)

        def body(cols):
            target[:, cols] = piece(cols) + z_rp[y_, :, cols] + z_rm[y_, :, cols]
        over_cols(body)

    row_total(1 - yl, o_ys)
    o_over = send(o_ys, o_yr, yn)
    row_total(yl, o_own)
    o_over.wait_recv()
    out[...] = (o_own[...] + o_yr[...]).astype(BF)
    next(grd_steps)
    for copy in stores:
        copy.wait()
    for copy in sent:
        copy.wait_send()


def forward(tokens, cotangent, gate_weight, up_weight, down_weight, keep_in, keep_out):
    hbm = pl.BlockSpec(memory_space=pl.ANY)
    vmem = pl.BlockSpec(memory_space=pltpu.VMEM)

    def bf(*shape):
        return pltpu.VMEM(shape, BF)

    def f32(*shape):
        return pltpu.VMEM(shape, F32)

    def ring(w):
        return [
            bf(512, w), bf(512, w), bf(512, w), bf(256, w), bf(256, w), bf(512, w), bf(512, w),
            bf(256, w), bf(256, w), f32(256, w),
        ]

    sds = jax.ShapeDtypeStruct
    return pl.pallas_call(
        forward_kernel,
        out_shape=(
            sds((128, 1024), BF), sds((2048, 1024), BF), sds((2048, 1024), BF),
            sds((2048, 896), BF), sds((2048, 1792), BF),
        ),
        in_specs=[vmem, vmem, hbm, hbm, hbm, vmem, vmem],
        out_specs=[vmem, hbm, hbm, hbm, hbm],
        scratch_shapes=[bf(1024, 1792), bf(896, 1024), bf(2048, 1024), bf(2048, 1024)]
        + ring(1792)
        + ring(896)
        + [bf(256, 896), bf(256, 1792), bf(2048, 896)]
        + [f32(8, 128, 1024), f32(8, 128, 1024)]
        + [f32(2, 128, 1024)] * 6
        + [f32(128, 1024)] * 3
        + [
            pltpu.SemaphoreType.DMA((SLOTS,)), pltpu.SemaphoreType.DMA((SLOTS,)),
            pltpu.SemaphoreType.DMA((8,)),
        ],
        compiler_params=pltpu.CompilerParams(
            collective_id=0, has_side_effects=True, vmem_limit_bytes=VMEM_LIMIT
        ),
    )(tokens, cotangent, gate_weight, up_weight, down_weight, keep_in, keep_out)


def expand(mask):
    return jnp.repeat(jnp.repeat(mask, BLK, axis=0), BLK, axis=1) > 0


def shards(tokens, gate_weight, up_weight, down_weight, input_mask, output_mask, cotangent):
    width = gate_weight.shape[1]
    lanes_in = jnp.repeat(input_mask.astype(F32), BLK, axis=1)
    lanes_out = jnp.repeat(output_mask.astype(F32), BLK, axis=1)
    output, tok_all, cot_all, hid_all, grd_all = forward(
        tokens, cotangent, gate_weight, up_weight, down_weight, lanes_in, lanes_out
    )
    keep_in, keep_out = expand(input_mask), expand(output_mask)
    outer = (((0,), (0,)), ((), ()))

    def grad(left, right, keep):
        full = lax.dot_general(left, right, outer, preferred_element_type=F32)
        return jnp.where(keep, full, jnp.zeros((), F32))

    grad_down = grad(hid_all, cot_all, keep_out)
    grad_gate = grad(tok_all, grd_all[:, :width], keep_in)
    grad_up = grad(tok_all, grd_all[:, width:], keep_in)
    return (output, grad_gate, grad_up, grad_down)


def solution(mesh):
    placed = (
        P("row", "col"), P("col", "row"), P("col", "row"), P("row", "col"),
        P("col", "row"), P("row", "col"), P("row", "col"),
    )
    return jax.shard_map(
        shards, mesh=mesh, in_specs=placed,
        out_specs=(P("row", "col"), P("col", "row"), P("col", "row"), P("row", "col")),
        check_vma=False,
    )
```

```python
import jax
import jax.numpy as jnp
from jax import lax
from jax.experimental import pallas as pl
from jax.experimental.pallas import tpu as pltpu
from jax.sharding import PartitionSpec as P

BLK = 128
BF = jnp.bfloat16
F32 = jnp.float32
MESH = pl.DeviceIdType.MESH
VMEM_LIMIT = 62 * 2**20
SLOTS = 112


def aligned(start, size, to=128):
    return pl.ds(pl.multiple_of(start, to), size)


def forward_kernel(
    tok, cot, gate_w, up_w, down_w, keep_in, keep_out,
    out, tok_hbm, cot_hbm, hid_hbm, gp_hbm, up_hbm,
    w_gate, w_up, w_down, tok_all, cot_all,
    g_s2, g_sp, g_sm, g_ia, g_ib, g_rp, g_rm, g_ys, g_yr, g_own,
    h_s2, h_sp, h_sm, h_ia, h_ib, h_rp, h_rm, h_ys, h_yr, h_own,
    u_ys, u_yr, u_s2, u_sp, u_sm, u_ia, u_ib, u_rp, u_rm, u_own,
    hid_own, gp_own, up_own, hid_all,
    c_s, c_r, z_s2, z_i, z_sp, z_sm, z_rp, z_rm, o_ys, o_yr, o_own,
    send_sem, recv_sem, local_sem,
):
    row = lax.axis_index("row")
    col = lax.axis_index("col")
    x, h = col // 2, col % 2
    yl, z, c = row // 8, (row // 2) % 4, row % 2

    def device(x_, h_, yl_, z_, c_):
        return (yl_ * 8 + z_ * 2 + c_, x_ * 2 + h_)

    xp = device((x + 1) % 4, h, yl, z, c)
    xm = device((x + 3) % 4, h, yl, z, c)
    yh = device(x, 1 - h, yl, z, c)
    yn = device(x, h, 1 - yl, z, c)
    zp = device(x, h, yl, (z + 1) % 4, c)
    zm = device(x, h, yl, (z + 3) % 4, c)
    co = device(x, h, yl, z, 1 - c)
    peers = (xp, xm, yh, yn, zp, zm, co)

    slot = [0]
    sent = []

    def send(src, dst, peer):
        i = slot[0]
        slot[0] += 1
        copy = pltpu.make_async_remote_copy(
            src_ref=src, dst_ref=dst, send_sem=send_sem.at[i], recv_sem=recv_sem.at[i],
            device_id=peer, device_id_type=MESH,
        )
        copy.start()
        sent.append(copy)
        return copy

    locals_ = [0]

    def local(src, dst):
        copy = pltpu.make_async_copy(src, dst, local_sem.at[locals_[0]])
        locals_[0] += 1
        copy.start()
        return copy

    loads = [local(gate_w, w_gate), local(up_w, w_up), local(down_w, w_down)]

    barrier = pltpu.get_barrier_semaphore()
    for peer in peers:
        pl.semaphore_signal(barrier, inc=1, device_id=peer, device_id_type=MESH)
    pl.semaphore_wait(barrier, len(peers))

    def block(yl_, z_, c_):
        return yl_ * 8 + z_ * 2 + c_

    def rows(b, part=0, size=128):
        return aligned(b * 128 + part * 64, size, 64)

    def gather_row(own, whole):
        me = block(yl, z, c)
        spot = whole.at[rows(me)]
        to_y = send(own, spot, yn)
        own_p, own_m = send(own, spot, zp), send(own, spot, zm)
        cores = [send(own, spot, co)]
        whole[rows(me), :] = own[...]
        yield
        to_y.wait_recv()
        spot = whole.at[rows(block(1 - yl, z, c))]
        mate_p, mate_m = send(spot, spot, zp), send(spot, spot, zm)
        cores.append(send(spot, spot, co))
        halves = []
        for y_, from_m, from_p in ((yl, own_p, own_m), (1 - yl, mate_p, mate_m)):
            from_m.wait_recv()
            b = block(y_, (z + 3) % 4, c)
            spot = whole.at[rows(b, 0, 64)]
            first = send(spot, spot, zp)
            spot = whole.at[rows(b)]
            cores.append(send(spot, spot, co))
            from_p.wait_recv()
            b = block(y_, (z + 1) % 4, c)
            spot = whole.at[rows(b, 1, 64)]
            second = send(spot, spot, zm)
            spot = whole.at[rows(b)]
            cores.append(send(spot, spot, co))
            halves.append((y_, first, second))
        yield
        for y_, first, second in halves:
            first.wait_recv()
            second.wait_recv()
            spot = whole.at[rows(block(y_, (z + 2) % 4, c))]
            cores.append(send(spot, spot, co))
        for copy in cores:
            copy.wait_recv()
        yield

    tok_steps = gather_row(tok, tok_all)
    cot_steps = gather_row(cot, cot_all)
    next(tok_steps)

    for copy in loads:
        copy.wait()
    @pl.loop(0, 8)
    def _(i):
        at = aligned(i * 128, 128)
        for j in range(7):
            cols = slice(j * 128, j * 128 + 128)
            kept_in = keep_in[i, j].astype(F32)
            w_gate[at, cols] = (w_gate[at, cols].astype(F32) * kept_in).astype(BF)
            w_up[at, cols] = (w_up[at, cols].astype(F32) * kept_in).astype(BF)

    @pl.loop(0, 7)
    def _(i):
        at = aligned(i * 128, 128)
        for j in range(8):
            cols = slice(j * 128, j * 128 + 128)
            kept_out = keep_out[i, j].astype(F32)
            w_down[at, cols] = (w_down[at, cols].astype(F32) * kept_out).astype(BF)

    next(tok_steps)
    next(cot_steps)
    next(tok_steps)
    stores = [local(tok_all, tok_hbm)]

    def tiles(body):
        @pl.loop(0, 3)
        def _(t):
            body(aligned(t * 256, 256, 256))

        body(pl.ds(768, 128))

    def product_of(lhs, rhs, transposed):
        def product(start, size, emit):
            at = aligned(start, size)

            def body(cols):
                if transposed:
                    v = lax.dot_general(
                        lhs[at, :], rhs[cols, :], (((1,), (1,)), ((), ())),
                        preferred_element_type=F32,
                    )
                else:
                    v = jnp.dot(lhs[at, :], rhs[:, cols], preferred_element_type=F32)
                emit(v, cols)
            tiles(body)
        return product

    gate_of = product_of(tok_all, w_gate, False)
    upper_of = product_of(tok_all, w_up, False)
    grad_of = product_of(cot_all, w_down, True)
    far, after, before = (x + 2) % 4, (x + 1) % 4, (x + 3) % 4

    def put(target, *terms):
        def emit(v, cols):
            for ref, at in terms:
                v = v + ref[at, cols].astype(F32)
            ref, at = target
            ref[at, cols] = v.astype(ref.dtype)
        return emit

    def reduce_x(product, s2, sp, sm, ia, ib, rp, rm, ys, yr, own):
        lo, hi, one = pl.ds(0, 256), pl.ds(256, 256), pl.ds(0, 256)
        product(far * 512, 256, put((s2, lo)))
        mid_a = send(s2.at[lo], ia, xp)
        product(far * 512 + 256, 256, put((s2, hi)))
        mid_b = send(s2.at[hi], ib, xm)
        yield
        product(after * 512 + 256, 256, put((sp, hi)))
        fin = [send(sp.at[hi], rp.at[hi], xp)]
        product(before * 512, 256, put((sm, lo)))
        fin.append(send(sm.at[lo], rm.at[lo], xm))
        yield
        mid_a.wait_recv()
        product(after * 512, 256, put((sp, lo), (ia, one)))
        fin.append(send(sp.at[lo], rp.at[lo], xp))
        mid_b.wait_recv()
        product(before * 512 + 256, 256, put((sm, hi), (ib, one)))
        fin.append(send(sm.at[hi], rm.at[hi], xm))
        yield
        for copy in fin:
            copy.wait_recv()

        def total(half, target):
            at = aligned(half * 256, 256, 256)
            product(x * 512 + half * 256, 256, put((target, one), (rp, at), (rm, at)))

        total(1 - h, ys)
        over = send(ys, yr, yh)
        total(h, own)
        yield
        over.wait_recv()
        yield

    def reduce_y(product, ys, yr, s2, sp, sm, ia, ib, rp, rm, own):
        chunks = (far, after, before, x)
        over = []
        lo, hi, one, two = pl.ds(0, 128), pl.ds(128, 128), pl.ds(0, 128), pl.ds(0, 256)

        def cross(k):
            at = pl.ds(k * 256, 256)
            product(chunks[k] * 512 + (1 - h) * 256, 256, put((ys, at)))
            over.append(send(ys.at[at], yr.at[at], yh))

        def mine(k, half):
            return chunks[k] * 512 + h * 256 + half * 128

        def came(k, half):
            return (yr, pl.ds(k * 256 + half * 128, 128))

        cross(0)
        yield
        for k in range(1, 4):
            cross(k)
        yield
        over[0].wait_recv()
        product(mine(0, 0), 256, put((s2, two), (yr, pl.ds(0, 256))))
        mid_a = send(s2.at[lo], ia, xp)
        mid_b = send(s2.at[hi], ib, xm)
        yield
        over[1].wait_recv()
        product(mine(1, 1), 128, put((sp, hi), came(1, 1)))
        fin = [send(sp.at[hi], rp.at[hi], xp)]
        yield
        over[2].wait_recv()
        product(mine(2, 0), 128, put((sm, lo), came(2, 0)))
        fin.append(send(sm.at[lo], rm.at[lo], xm))
        mid_a.wait_recv()
        product(mine(1, 0), 128, put((sp, lo), came(1, 0), (ia, one)))
        fin.append(send(sp.at[lo], rp.at[lo], xp))
        mid_b.wait_recv()
        product(mine(2, 1), 128, put((sm, hi), came(2, 1), (ib, one)))
        fin.append(send(sm.at[hi], rm.at[hi], xm))
        yield
        over[3].wait_recv()
        for copy in fin:
            copy.wait_recv()
        product(mine(3, 0), 256, put((own, two), (yr, pl.ds(768, 256)), (rp, two), (rm, two)))
        yield

    def spot_in(whole, x_, h_, part=0, size=256):
        return whole.at[aligned(x_ * 512 + h_ * 256 + part * 128, size)]

    def gather_y(own, whole, arrived=None):
        def came(x_, h_):
            if arrived is not None:
                arrived(x_, h_)

        spot = spot_in(whole, x, h)
        to_y = send(own, spot, yh)
        mine = local(own, spot)
        yield
        own_p, own_m = send(own, spot, xp), send(own, spot, xm)
        mine.wait()
        came(x, h)
        yield
        to_y.wait_recv()
        spot = spot_in(whole, x, 1 - h)
        mate_p, mate_m = send(spot, spot, xp), send(spot, spot, xm)
        came(x, 1 - h)
        yield
        halves = []
        for h_, from_m, from_p in ((h, own_p, own_m), (1 - h, mate_p, mate_m)):
            from_m.wait_recv()
            spot = spot_in(whole, before, h_, 0, 128)
            halves.append(send(spot, spot, xp))
            from_p.wait_recv()
            spot = spot_in(whole, after, h_, 1, 128)
            halves.append(send(spot, spot, xm))
            came(before, h_)
            came(after, h_)
            yield
        for i, h_ in enumerate((h, 1 - h)):
            halves[2 * i].wait_recv()
            halves[2 * i + 1].wait_recv()
            came(far, h_)
        yield

    def gather_x(own, whole):
        spot = spot_in(whole, x, h)
        own_p, own_m = send(own, spot, xp), send(own, spot, xm)
        mine = local(own, spot)
        yield
        over = [send(own, spot, yh)]
        yield
        own_p.wait_recv()
        spot = spot_in(whole, before, h, 0, 128)
        half_a = send(spot, spot, xp)
        spot = spot_in(whole, before, h)
        over.append(send(spot, spot, yh))
        own_m.wait_recv()
        spot = spot_in(whole, after, h, 1, 128)
        half_b = send(spot, spot, xm)
        spot = spot_in(whole, after, h)
        over.append(send(spot, spot, yh))
        yield
        half_a.wait_recv()
        half_b.wait_recv()
        spot = spot_in(whole, far, h)
        over.append(send(spot, spot, yh))
        yield
        for copy in over:
            copy.wait_recv()
        mine.wait()
        yield

    core = []

    def cross_core(x_, h_):
        pair = x_ * 2 + h_

        @pl.loop(0, 4)
        def _(t):
            cols = aligned(t * 256, 256, 256)
            c_s[pair, :, cols] = jnp.dot(
                hid_all[rows(pair * 2 + 1 - c), :], w_down[:, cols], preferred_element_type=F32
            )
        core.append(send(c_s.at[pair], c_r.at[pair], co))

    gate = reduce_x(gate_of, g_s2, g_sp, g_sm, g_ia, g_ib, g_rp, g_rm, g_ys, g_yr, g_own)
    upper = reduce_y(upper_of, u_ys, u_yr, u_s2, u_sp, u_sm, u_ia, u_ib, u_rp, u_rm, u_own)
    grad = reduce_x(grad_of, h_s2, h_sp, h_sm, h_ia, h_ib, h_rp, h_rm, h_ys, h_yr, h_own)
    next(gate)
    next(upper)
    next(gate)
    next(upper)
    next(cot_steps)
    next(cot_steps)
    stores.append(local(cot_all, cot_hbm))
    next(upper)
    next(gate)
    next(upper)
    next(grad)
    next(grad)
    next(upper)
    next(gate)
    next(grad)
    next(upper)
    next(gate)

    @pl.loop(0, 16)
    def _(t):
        at = aligned(t * 16, 16, 16)
        gate_v = g_own[at, :] + g_yr[at, :].astype(F32)
        upper_v = u_own[at, :]
        sigma = 1.0 / (1.0 + jnp.exp(-gate_v))
        swish = gate_v * sigma
        hid_own[at, :] = (swish * upper_v).astype(BF)
        g_own[at, :] = upper_v * sigma * (1.0 + gate_v * (1.0 - sigma))
        u_own[at, :] = swish

    hid = gather_y(hid_own, hid_all, cross_core)
    next(hid)
    next(hid)
    next(grad)
    next(hid)
    next(hid)
    next(grad)

    @pl.loop(0, 16)
    def _(t):
        at = aligned(t * 16, 16, 16)
        grad_v = h_own[at, :] + h_yr[at, :].astype(F32)
        gp_own[at, :] = (grad_v * g_own[at, :]).astype(BF)
        up_own[at, :] = (grad_v * u_own[at, :]).astype(BF)

    gp = gather_x(gp_own, gp_hbm)
    up = gather_y(up_own, up_hbm)
    next(up)
    next(gp)
    next(gp)
    next(hid)
    next(up)
    next(hid)
    next(up)
    next(gp)
    stores.append(local(hid_all, hid_hbm))

    def kept(yl_, z_):
        def piece(cols):
            part = jnp.dot(
                hid_all[rows(block(yl_, z_, c)), :], w_down[:, cols], preferred_element_type=F32
            )
            return part + c_r[yl_ * 4 + z_, :, cols]
        return piece

    def over_cols(body):
        @pl.loop(0, 4)
        def _(t):
            body(aligned(t * 256, 256, 256))

    for copy in core:
        copy.wait_recv()
    z_far, z_after, z_before = (z + 2) % 4, (z + 1) % 4, (z + 3) % 4

    def ring_piece(y_, z_, target, inc=None):
        piece = kept(y_, z_)

        def body(cols):
            v = piece(cols)
            if inc is not None:
                v = v + inc[:, cols]
            target[:, cols] = v
        over_cols(body)

    ring_piece(0, z_far, z_s2.at[0])
    z_mid_a = send(z_s2.at[0], z_i.at[0], zp)
    ring_piece(1, z_far, z_s2.at[1])
    z_mid_b = send(z_s2.at[1], z_i.at[1], zm)
    ring_piece(1, z_after, z_sp.at[1])
    z_fin = [send(z_sp.at[1], z_rp.at[1], zp)]
    ring_piece(0, z_before, z_sm.at[0])
    z_fin.append(send(z_sm.at[0], z_rm.at[0], zm))
    next(up)
    next(gp)
    z_mid_a.wait_recv()
    ring_piece(0, z_after, z_sp.at[0], z_i.at[0])
    z_fin.append(send(z_sp.at[0], z_rp.at[0], zp))
    z_mid_b.wait_recv()
    ring_piece(1, z_before, z_sm.at[1], z_i.at[1])
    z_fin.append(send(z_sm.at[1], z_rm.at[1], zm))
    next(up)
    for copy in z_fin:
        copy.wait_recv()

    def row_total(y_, target):
        piece = kept(y_, z)

        def body(cols):
            target[:, cols] = piece(cols) + z_rp[y_, :, cols] + z_rm[y_, :, cols]
        over_cols(body)

    row_total(1 - yl, o_ys)
    o_over = send(o_ys, o_yr, yn)
    row_total(yl, o_own)
    o_over.wait_recv()
    out[...] = (o_own[...] + o_yr[...]).astype(BF)
    next(up)
    next(gp)
    for copy in stores:
        copy.wait()
    for copy in sent:
        copy.wait_send()


def forward(tokens, cotangent, gate_weight, up_weight, down_weight, keep_in, keep_out):
    hbm = pl.BlockSpec(memory_space=pl.ANY)
    vmem = pl.BlockSpec(memory_space=pltpu.VMEM)

    def bf(*shape):
        return pltpu.VMEM(shape, BF)

    def f32(*shape):
        return pltpu.VMEM(shape, F32)

    def ring(n):
        return [bf(n, 896)] * 3 + [bf(n // 2, 896)] * 2 + [bf(n, 896)] * 2

    def ring_y():
        return ring(512) + [bf(256, 896), bf(256, 896), f32(256, 896)]

    smem = pl.BlockSpec(memory_space=pltpu.SMEM)
    sds = jax.ShapeDtypeStruct
    return pl.pallas_call(
        forward_kernel,
        out_shape=(
            sds((128, 1024), BF), sds((2048, 1024), BF), sds((2048, 1024), BF),
            sds((2048, 896), BF), sds((2048, 896), BF), sds((2048, 896), BF),
        ),
        in_specs=[vmem, vmem, hbm, hbm, hbm, smem, smem],
        out_specs=[vmem, hbm, hbm, hbm, hbm, hbm],
        scratch_shapes=[bf(1024, 896), bf(1024, 896), bf(896, 1024), bf(2048, 1024), bf(2048, 1024)]
        + ring_y()
        + ring_y()
        + [bf(1024, 896), bf(1024, 896)] + ring(256) + [f32(256, 896)]
        + [bf(256, 896)] * 3 + [bf(2048, 896)]
        + [f32(8, 128, 1024), f32(8, 128, 1024)]
        + [f32(2, 128, 1024)] * 6
        + [f32(128, 1024)] * 3
        + [
            pltpu.SemaphoreType.DMA((SLOTS,)), pltpu.SemaphoreType.DMA((SLOTS,)),
            pltpu.SemaphoreType.DMA((12,)),
        ],
        compiler_params=pltpu.CompilerParams(
            collective_id=0, has_side_effects=True, vmem_limit_bytes=VMEM_LIMIT
        ),
    )(tokens, cotangent, gate_weight, up_weight, down_weight, keep_in, keep_out)


def expand(mask):
    return jnp.repeat(jnp.repeat(mask, BLK, axis=0), BLK, axis=1) > 0


def shards(tokens, gate_weight, up_weight, down_weight, input_mask, output_mask, cotangent):
    output, tok_all, cot_all, hid_all, gp_all, up_all = forward(
        tokens, cotangent, gate_weight, up_weight, down_weight, input_mask, output_mask
    )
    keep_in, keep_out = expand(input_mask), expand(output_mask)
    outer = (((0,), (0,)), ((), ()))

    def grad(left, right, keep):
        full = lax.dot_general(left, right, outer, preferred_element_type=F32)
        return jnp.where(keep, full, jnp.zeros((), F32))

    grad_down = grad(hid_all, cot_all, keep_out)
    grad_gate = grad(tok_all, gp_all, keep_in)
    grad_up = grad(tok_all, up_all, keep_in)
    return (output, grad_gate, grad_up, grad_down)


def solution(mesh):
    placed = (
        P("row", "col"), P("col", "row"), P("col", "row"), P("row", "col"),
        P("col", "row"), P("row", "col"), P("row", "col"),
    )
    return jax.shard_map(
        shards, mesh=mesh, in_specs=placed,
        out_specs=(P("row", "col"), P("col", "row"), P("col", "row"), P("row", "col")),
        check_vma=False,
    )
```

```python
import jax
import jax.numpy as jnp
from jax import lax
from jax.experimental import pallas as pl
from jax.experimental.pallas import tpu as pltpu
from jax.sharding import PartitionSpec as P

BF = jnp.bfloat16
F32 = jnp.float32
MESH = pl.DeviceIdType.MESH
VMEM_LIMIT = 62 * 2**20
SLOTS = 112


def aligned(start, size, to=128):
    return pl.ds(pl.multiple_of(start, to), size)


def forward_kernel(
    tok, cot, gate_w, up_w, down_w, keep_in, keep_out,
    out, tok_t_hbm, down_hbm, gp_hbm, up_hbm,
    w_gate, w_up, w_down, tok_all, cot_all,
    g_s2, g_sp, g_sm, g_ia, g_ib, g_rp, g_rm, g_ys, g_yr, g_own,
    h_s2, h_sp, h_sm, h_ia, h_ib, h_rp, h_rm, h_ys, h_yr, h_own,
    u_ys, u_yr, u_s2, u_sp, u_sm, u_ia, u_ib, u_rp, u_rm, u_own,
    hid_own, gp_own, up_own, hid_all,
    c_s, c_r, z_s2, z_i, z_sp, z_sm, z_rp, z_rm, o_ys, o_yr, o_own, tok_t, down_t,
    send_sem, recv_sem, local_sem,
):
    row = lax.axis_index("row")
    col = lax.axis_index("col")
    x, h = col // 2, col % 2
    yl, z, c = row // 8, (row // 2) % 4, row % 2

    def device(x_, h_, yl_, z_, c_):
        return (yl_ * 8 + z_ * 2 + c_, x_ * 2 + h_)

    xp = device((x + 1) % 4, h, yl, z, c)
    xm = device((x + 3) % 4, h, yl, z, c)
    yh = device(x, 1 - h, yl, z, c)
    yn = device(x, h, 1 - yl, z, c)
    zp = device(x, h, yl, (z + 1) % 4, c)
    zm = device(x, h, yl, (z + 3) % 4, c)
    co = device(x, h, yl, z, 1 - c)
    peers = (xp, xm, yh, yn, zp, zm, co)

    slot = [0]
    sent = []

    def send(src, dst, peer):
        i = slot[0]
        slot[0] += 1
        copy = pltpu.make_async_remote_copy(
            src_ref=src, dst_ref=dst, send_sem=send_sem.at[i], recv_sem=recv_sem.at[i],
            device_id=peer, device_id_type=MESH,
        )
        copy.start()
        sent.append(copy)
        return copy

    locals_ = [0]

    def local(src, dst):
        copy = pltpu.make_async_copy(src, dst, local_sem.at[locals_[0]])
        locals_[0] += 1
        copy.start()
        return copy

    loads = [local(gate_w, w_gate), local(up_w, w_up), local(down_w, w_down)]

    barrier = pltpu.get_barrier_semaphore()
    for peer in peers:
        pl.semaphore_signal(barrier, inc=1, device_id=peer, device_id_type=MESH)
    pl.semaphore_wait(barrier, len(peers))

    def block(yl_, z_, c_):
        return yl_ * 8 + z_ * 2 + c_

    def rows(b, part=0, size=128):
        return aligned(b * 128 + part * 64, size, 64)

    def gather_row(own, whole):
        me = block(yl, z, c)
        spot = whole.at[rows(me)]
        to_y = send(own, spot, yn)
        own_p, own_m = send(own, spot, zp), send(own, spot, zm)
        cores = [send(own, spot, co)]
        whole[rows(me), :] = own[...]
        yield
        to_y.wait_recv()
        spot = whole.at[rows(block(1 - yl, z, c))]
        mate_p, mate_m = send(spot, spot, zp), send(spot, spot, zm)
        cores.append(send(spot, spot, co))
        halves = []
        for y_, from_m, from_p in ((yl, own_p, own_m), (1 - yl, mate_p, mate_m)):
            from_m.wait_recv()
            b = block(y_, (z + 3) % 4, c)
            spot = whole.at[rows(b, 0, 64)]
            first = send(spot, spot, zp)
            spot = whole.at[rows(b)]
            cores.append(send(spot, spot, co))
            from_p.wait_recv()
            b = block(y_, (z + 1) % 4, c)
            spot = whole.at[rows(b, 1, 64)]
            second = send(spot, spot, zm)
            spot = whole.at[rows(b)]
            cores.append(send(spot, spot, co))
            halves.append((y_, first, second))
        yield
        for y_, first, second in halves:
            first.wait_recv()
            second.wait_recv()
            spot = whole.at[rows(block(y_, (z + 2) % 4, c))]
            cores.append(send(spot, spot, co))
        for copy in cores:
            copy.wait_recv()
        yield

    tok_steps = gather_row(tok, tok_all)
    cot_steps = gather_row(cot, cot_all)
    next(tok_steps)

    for copy in loads:
        copy.wait()
    @pl.loop(0, 8)
    def _(i):
        at = aligned(i * 128, 128)
        for j in range(7):
            cols = slice(j * 128, j * 128 + 128)
            kept_in = keep_in[i, j].astype(F32)
            w_gate[at, cols] = (w_gate[at, cols].astype(F32) * kept_in).astype(BF)
            w_up[at, cols] = (w_up[at, cols].astype(F32) * kept_in).astype(BF)

    @pl.loop(0, 7)
    def _(i):
        at = aligned(i * 128, 128)
        for j in range(8):
            cols = slice(j * 128, j * 128 + 128)
            kept_out = keep_out[i, j].astype(F32)
            w_down[at, cols] = (w_down[at, cols].astype(F32) * kept_out).astype(BF)

    next(tok_steps)
    next(cot_steps)
    next(tok_steps)
    flips = []

    def flip(first, last):
        for i in range(first, last):
            if len(flips) >= 2:
                flips[-2].wait()
            at = slice(i * 128, i * 128 + 128)
            tok_t[i % 2] = tok_all[:, at].T
            flips.append(local(tok_t.at[i % 2], tok_t_hbm.at[at]))

    downs = []

    def down_grad(i):
        if len(downs) >= 2:
            downs[-2].wait()
        units = slice(i * 128, i * 128 + 128)
        left = hid_all[:, units].T

        @pl.loop(0, 4)
        def _(t):
            v = jnp.dot(left, cot_all[:, aligned(t * 256, 256, 256)], preferred_element_type=F32)
            for j in range(2):
                kept_out = keep_out[i, 2 * t + j].astype(F32)
                down_t[i % 2, :, aligned(t * 256 + j * 128, 128)] = (
                    v[:, j * 128 : j * 128 + 128] * kept_out
                )
        downs.append(local(down_t.at[i % 2], down_hbm.at[units]))

    def tiles(body):
        @pl.loop(0, 3)
        def _(t):
            body(aligned(t * 256, 256, 256))

        body(pl.ds(768, 128))

    def product_of(lhs, rhs, transposed):
        def product(start, size, emit):
            at = aligned(start, size)

            def body(cols):
                if transposed:
                    v = lax.dot_general(
                        lhs[at, :], rhs[cols, :], (((1,), (1,)), ((), ())),
                        preferred_element_type=F32,
                    )
                else:
                    v = jnp.dot(lhs[at, :], rhs[:, cols], preferred_element_type=F32)
                emit(v, cols)
            tiles(body)
        return product

    gate_of = product_of(tok_all, w_gate, False)
    upper_of = product_of(tok_all, w_up, False)
    grad_of = product_of(cot_all, w_down, True)
    far, after, before = (x + 2) % 4, (x + 1) % 4, (x + 3) % 4

    def put(target, *terms):
        def emit(v, cols):
            for ref, at in terms:
                v = v + ref[at, cols].astype(F32)
            ref, at = target
            ref[at, cols] = v.astype(ref.dtype)
        return emit

    def reduce_x(product, s2, sp, sm, ia, ib, rp, rm, ys, yr, own):
        lo, hi, one = pl.ds(0, 256), pl.ds(256, 256), pl.ds(0, 256)
        product(far * 512, 256, put((s2, lo)))
        mid_a = send(s2.at[lo], ia, xp)
        product(far * 512 + 256, 256, put((s2, hi)))
        mid_b = send(s2.at[hi], ib, xm)
        yield
        product(after * 512 + 256, 256, put((sp, hi)))
        fin = [send(sp.at[hi], rp.at[hi], xp)]
        product(before * 512, 256, put((sm, lo)))
        fin.append(send(sm.at[lo], rm.at[lo], xm))
        yield
        mid_a.wait_recv()
        product(after * 512, 256, put((sp, lo), (ia, one)))
        fin.append(send(sp.at[lo], rp.at[lo], xp))
        mid_b.wait_recv()
        product(before * 512 + 256, 256, put((sm, hi), (ib, one)))
        fin.append(send(sm.at[hi], rm.at[hi], xm))
        yield
        for copy in fin:
            copy.wait_recv()

        def total(half, target):
            at = aligned(half * 256, 256, 256)
            product(x * 512 + half * 256, 256, put((target, one), (rp, at), (rm, at)))

        total(1 - h, ys)
        over = send(ys, yr, yh)
        total(h, own)
        yield
        over.wait_recv()
        yield

    def reduce_y(product, ys, yr, s2, sp, sm, ia, ib, rp, rm, own):
        chunks = (far, after, before, x)
        over = []
        lo, hi, one, two = pl.ds(0, 128), pl.ds(128, 128), pl.ds(0, 128), pl.ds(0, 256)

        def cross(k):
            at = pl.ds(k * 256, 256)
            product(chunks[k] * 512 + (1 - h) * 256, 256, put((ys, at)))
            over.append(send(ys.at[at], yr.at[at], yh))

        def mine(k, half):
            return chunks[k] * 512 + h * 256 + half * 128

        def came(k, half):
            return (yr, pl.ds(k * 256 + half * 128, 128))

        cross(0)
        yield
        for k in range(1, 4):
            cross(k)
        yield
        over[0].wait_recv()
        product(mine(0, 0), 256, put((s2, two), (yr, pl.ds(0, 256))))
        mid_a = send(s2.at[lo], ia, xp)
        mid_b = send(s2.at[hi], ib, xm)
        yield
        over[1].wait_recv()
        product(mine(1, 1), 128, put((sp, hi), came(1, 1)))
        fin = [send(sp.at[hi], rp.at[hi], xp)]
        yield
        over[2].wait_recv()
        product(mine(2, 0), 128, put((sm, lo), came(2, 0)))
        fin.append(send(sm.at[lo], rm.at[lo], xm))
        mid_a.wait_recv()
        product(mine(1, 0), 128, put((sp, lo), came(1, 0), (ia, one)))
        fin.append(send(sp.at[lo], rp.at[lo], xp))
        mid_b.wait_recv()
        product(mine(2, 1), 128, put((sm, hi), came(2, 1), (ib, one)))
        fin.append(send(sm.at[hi], rm.at[hi], xm))
        yield
        over[3].wait_recv()
        for copy in fin:
            copy.wait_recv()
        product(mine(3, 0), 256, put((own, two), (yr, pl.ds(768, 256)), (rp, two), (rm, two)))
        yield

    def spot_in(whole, x_, h_, part=0, size=256):
        return whole.at[aligned(x_ * 512 + h_ * 256 + part * 128, size)]

    def gather_y(own, whole, arrived=None):
        def came(x_, h_):
            if arrived is not None:
                arrived(x_, h_)

        spot = spot_in(whole, x, h)
        to_y = send(own, spot, yh)
        mine = local(own, spot)
        yield
        own_p, own_m = send(own, spot, xp), send(own, spot, xm)
        mine.wait()
        came(x, h)
        yield
        to_y.wait_recv()
        spot = spot_in(whole, x, 1 - h)
        mate_p, mate_m = send(spot, spot, xp), send(spot, spot, xm)
        came(x, 1 - h)
        yield
        halves = []
        for h_, from_m, from_p in ((h, own_p, own_m), (1 - h, mate_p, mate_m)):
            from_m.wait_recv()
            spot = spot_in(whole, before, h_, 0, 128)
            halves.append(send(spot, spot, xp))
            from_p.wait_recv()
            spot = spot_in(whole, after, h_, 1, 128)
            halves.append(send(spot, spot, xm))
            came(before, h_)
            came(after, h_)
            yield
        for i, h_ in enumerate((h, 1 - h)):
            halves[2 * i].wait_recv()
            halves[2 * i + 1].wait_recv()
            came(far, h_)
        yield

    def gather_x(own, whole):
        spot = spot_in(whole, x, h)
        own_p, own_m = send(own, spot, xp), send(own, spot, xm)
        mine = local(own, spot)
        yield
        over = [send(own, spot, yh)]
        yield
        own_p.wait_recv()
        spot = spot_in(whole, before, h, 0, 128)
        half_a = send(spot, spot, xp)
        spot = spot_in(whole, before, h)
        over.append(send(spot, spot, yh))
        own_m.wait_recv()
        spot = spot_in(whole, after, h, 1, 128)
        half_b = send(spot, spot, xm)
        spot = spot_in(whole, after, h)
        over.append(send(spot, spot, yh))
        yield
        half_a.wait_recv()
        half_b.wait_recv()
        spot = spot_in(whole, far, h)
        over.append(send(spot, spot, yh))
        yield
        for copy in over:
            copy.wait_recv()
        mine.wait()
        yield

    core = []

    def cross_core(x_, h_):
        pair = x_ * 2 + h_

        @pl.loop(0, 4)
        def _(t):
            cols = aligned(t * 256, 256, 256)
            c_s[pair, :, cols] = jnp.dot(
                hid_all[rows(pair * 2 + 1 - c), :], w_down[:, cols], preferred_element_type=F32
            )
        core.append(send(c_s.at[pair], c_r.at[pair], co))

    gate = reduce_x(gate_of, g_s2, g_sp, g_sm, g_ia, g_ib, g_rp, g_rm, g_ys, g_yr, g_own)
    upper = reduce_y(upper_of, u_ys, u_yr, u_s2, u_sp, u_sm, u_ia, u_ib, u_rp, u_rm, u_own)
    grad = reduce_x(grad_of, h_s2, h_sp, h_sm, h_ia, h_ib, h_rp, h_rm, h_ys, h_yr, h_own)
    next(gate)
    next(upper)
    next(gate)
    next(upper)
    next(cot_steps)
    flip(0, 2)
    next(cot_steps)
    next(upper)
    next(gate)
    next(upper)
    next(grad)
    next(grad)
    flip(2, 4)
    next(upper)
    flip(4, 6)
    next(gate)
    flip(6, 8)
    next(grad)
    next(upper)
    next(gate)

    @pl.loop(0, 16)
    def _(t):
        at = aligned(t * 16, 16, 16)
        gate_v = g_own[at, :] + g_yr[at, :].astype(F32)
        upper_v = u_own[at, :]
        sigma = 1.0 / (1.0 + jnp.exp(-gate_v))
        swish = gate_v * sigma
        hid_own[at, :] = (swish * upper_v).astype(BF)
        g_own[at, :] = upper_v * sigma * (1.0 + gate_v * (1.0 - sigma))
        u_own[at, :] = swish

    hid = gather_y(hid_own, hid_all, cross_core)
    next(hid)
    next(hid)
    next(grad)
    next(hid)
    next(hid)
    next(grad)

    @pl.loop(0, 16)
    def _(t):
        at = aligned(t * 16, 16, 16)
        grad_v = h_own[at, :] + h_yr[at, :].astype(F32)
        gp_own[at, :] = (grad_v * g_own[at, :]).astype(BF)
        up_own[at, :] = (grad_v * u_own[at, :]).astype(BF)

    gp = gather_x(gp_own, gp_hbm)
    up = gather_y(up_own, up_hbm)
    next(up)
    next(gp)
    next(gp)
    next(hid)
    next(up)
    next(hid)
    next(up)
    next(gp)

    def kept(yl_, z_):
        def piece(cols):
            part = jnp.dot(
                hid_all[rows(block(yl_, z_, c)), :], w_down[:, cols], preferred_element_type=F32
            )
            return part + c_r[yl_ * 4 + z_, :, cols]
        return piece

    def over_cols(body):
        @pl.loop(0, 4)
        def _(t):
            body(aligned(t * 256, 256, 256))

    down_grad(0)
    for copy in core:
        copy.wait_recv()
    z_far, z_after, z_before = (z + 2) % 4, (z + 1) % 4, (z + 3) % 4

    def ring_piece(y_, z_, target, inc=None):
        piece = kept(y_, z_)

        def body(cols):
            v = piece(cols)
            if inc is not None:
                v = v + inc[:, cols]
            target[:, cols] = v
        over_cols(body)

    ring_piece(0, z_far, z_s2.at[0])
    z_mid_a = send(z_s2.at[0], z_i.at[0], zp)
    ring_piece(1, z_far, z_s2.at[1])
    z_mid_b = send(z_s2.at[1], z_i.at[1], zm)
    ring_piece(1, z_after, z_sp.at[1])
    z_fin = [send(z_sp.at[1], z_rp.at[1], zp)]
    ring_piece(0, z_before, z_sm.at[0])
    z_fin.append(send(z_sm.at[0], z_rm.at[0], zm))
    next(up)
    next(gp)
    down_grad(1)
    down_grad(2)
    z_mid_a.wait_recv()
    ring_piece(0, z_after, z_sp.at[0], z_i.at[0])
    z_fin.append(send(z_sp.at[0], z_rp.at[0], zp))
    z_mid_b.wait_recv()
    ring_piece(1, z_before, z_sm.at[1], z_i.at[1])
    z_fin.append(send(z_sm.at[1], z_rm.at[1], zm))
    down_grad(3)
    down_grad(4)
    next(up)
    down_grad(5)
    down_grad(6)
    for copy in z_fin:
        copy.wait_recv()

    def row_total(y_, target):
        piece = kept(y_, z)

        def body(cols):
            target[:, cols] = piece(cols) + z_rp[y_, :, cols] + z_rm[y_, :, cols]
        over_cols(body)

    row_total(1 - yl, o_ys)
    o_over = send(o_ys, o_yr, yn)
    row_total(yl, o_own)
    o_over.wait_recv()
    out[...] = (o_own[...] + o_yr[...]).astype(BF)
    next(up)
    next(gp)
    for copy in flips[-2:] + downs[-2:]:
        copy.wait()
    for copy in sent:
        copy.wait_send()


def forward(tokens, cotangent, gate_weight, up_weight, down_weight, keep_in, keep_out):
    hbm = pl.BlockSpec(memory_space=pl.ANY)
    vmem = pl.BlockSpec(memory_space=pltpu.VMEM)

    def bf(*shape):
        return pltpu.VMEM(shape, BF)

    def f32(*shape):
        return pltpu.VMEM(shape, F32)

    def ring(n):
        return [bf(n, 896)] * 3 + [bf(n // 2, 896)] * 2 + [bf(n, 896)] * 2

    def ring_y():
        return ring(512) + [bf(256, 896), bf(256, 896), f32(256, 896)]

    smem = pl.BlockSpec(memory_space=pltpu.SMEM)
    sds = jax.ShapeDtypeStruct
    return pl.pallas_call(
        forward_kernel,
        out_shape=(
            sds((128, 1024), BF), sds((1024, 2048), BF), sds((896, 1024), F32),
            sds((2048, 896), BF), sds((2048, 896), BF),
        ),
        in_specs=[vmem, vmem, hbm, hbm, hbm, smem, smem],
        out_specs=[vmem, hbm, hbm, hbm, hbm],
        scratch_shapes=[bf(1024, 896), bf(1024, 896), bf(896, 1024), bf(2048, 1024), bf(2048, 1024)]
        + ring_y()
        + ring_y()
        + [bf(1024, 896), bf(1024, 896)] + ring(256) + [f32(256, 896)]
        + [bf(256, 896)] * 3 + [bf(2048, 896)]
        + [f32(8, 128, 1024), f32(8, 128, 1024)]
        + [f32(2, 128, 1024)] * 6
        + [f32(128, 1024)] * 3
        + [bf(2, 128, 2048), f32(2, 128, 1024)]
        + [
            pltpu.SemaphoreType.DMA((SLOTS,)), pltpu.SemaphoreType.DMA((SLOTS,)),
            pltpu.SemaphoreType.DMA((24,)),
        ],
        compiler_params=pltpu.CompilerParams(
            collective_id=0, has_side_effects=True, vmem_limit_bytes=VMEM_LIMIT
        ),
    )(tokens, cotangent, gate_weight, up_weight, down_weight, keep_in, keep_out)


def input_grads_kernel(keep_in, tok_t, gp, up, gate_out, up_out):
    i = pl.program_id(0)

    def one(grads, target):
        def tile(cols, blocks, first):
            v = jnp.dot(tok_t[...], grads[:, cols], preferred_element_type=F32)
            for a in range(2):
                for b in range(blocks):
                    kept_in = keep_in[2 * i + a, first + b].astype(F32)
                    at = slice(a * 128, a * 128 + 128)
                    target[at, (first + b) * 128 : (first + b) * 128 + 128] = (
                        v[at, b * 128 : b * 128 + 128] * kept_in
                    )
        for t in range(3):
            tile(slice(t * 256, t * 256 + 256), 2, 2 * t)
        tile(slice(768, 896), 1, 6)

    one(gp, gate_out)
    one(up, up_out)


def input_grads(keep_in, tok_t, gp, up):
    whole = pl.BlockSpec((2048, 896), lambda i: (0, 0), pipeline_mode=pl.Buffered(1))
    piece = pl.BlockSpec((256, 896), lambda i: (i, 0))
    return pl.pallas_call(
        input_grads_kernel,
        grid=(4,),
        out_shape=(jax.ShapeDtypeStruct((1024, 896), F32),) * 2,
        in_specs=[
            pl.BlockSpec(memory_space=pltpu.SMEM),
            pl.BlockSpec((256, 2048), lambda i: (i, 0)), whole, whole,
        ],
        out_specs=[piece, piece],
        compiler_params=pltpu.CompilerParams(vmem_limit_bytes=40 * 2**20),
        cost_estimate=pl.CostEstimate(
            flops=4 * 2048 * 1024 * 896, bytes_accessed=20 * 2**20, transcendentals=0
        ),
    )(keep_in, tok_t, gp, up)


def shards(tokens, gate_weight, up_weight, down_weight, input_mask, output_mask, cotangent):
    output, tok_t, grad_down, gp, up = forward(
        tokens, cotangent, gate_weight, up_weight, down_weight, input_mask, output_mask
    )
    grad_gate, grad_up = input_grads(input_mask, tok_t, gp, up)
    return (output, grad_gate, grad_up, grad_down)


def solution(mesh):
    placed = (
        P("row", "col"), P("col", "row"), P("col", "row"), P("row", "col"),
        P("col", "row"), P("row", "col"), P("row", "col"),
    )
    return jax.shard_map(
        shards, mesh=mesh, in_specs=placed,
        out_specs=(P("row", "col"), P("col", "row"), P("col", "row"), P("row", "col")),
        check_vma=False,
    )
```

```python
import jax
import jax.numpy as jnp
from jax import lax
from jax.experimental import pallas as pl
from jax.experimental.pallas import tpu as pltpu
from jax.sharding import PartitionSpec as P

BF = jnp.bfloat16
F32 = jnp.float32
MESH = pl.DeviceIdType.MESH
VMEM_LIMIT = 62 * 2**20
SLOTS = 112


def aligned(start, size, to=128):
    return pl.ds(pl.multiple_of(start, to), size)


def forward_kernel(
    tok, cot, gate_w, up_w, down_w, keep_in, keep_out,
    out, tok_t_hbm, down_hbm, gp_hbm, up_hbm,
    w_gate, w_up, w_down, tok_all, cot_all,
    g_s2, g_sp, g_sm, g_ia, g_ib, g_rp, g_rm, g_ys, g_yr, g_own,
    h_s2, h_sp, h_sm, h_ia, h_ib, h_rp, h_rm, h_ys, h_yr, h_own,
    u_ys, u_yr, u_s2, u_sp, u_sm, u_ia, u_ib, u_rp, u_rm, u_own,
    hid_own, gp_own, up_own, hid_all,
    c_s, c_r, z_s2, z_i, z_sp, z_sm, z_rp, z_rm, o_ys, o_yr, o_own, tok_t, down_t,
    send_sem, recv_sem, local_sem,
):
    row = lax.axis_index("row")
    col = lax.axis_index("col")
    x, h = col // 2, col % 2
    yl, z, c = row // 8, (row // 2) % 4, row % 2

    def device(x_, h_, yl_, z_, c_):
        return (yl_ * 8 + z_ * 2 + c_, x_ * 2 + h_)

    xp = device((x + 1) % 4, h, yl, z, c)
    xm = device((x + 3) % 4, h, yl, z, c)
    yh = device(x, 1 - h, yl, z, c)
    yn = device(x, h, 1 - yl, z, c)
    zp = device(x, h, yl, (z + 1) % 4, c)
    zm = device(x, h, yl, (z + 3) % 4, c)
    co = device(x, h, yl, z, 1 - c)
    peers = (xp, xm, yh, yn, zp, zm, co)

    slot = [0]
    sent = []

    def send(src, dst, peer):
        i = slot[0]
        slot[0] += 1
        copy = pltpu.make_async_remote_copy(
            src_ref=src, dst_ref=dst, send_sem=send_sem.at[i], recv_sem=recv_sem.at[i],
            device_id=peer, device_id_type=MESH,
        )
        copy.start()
        sent.append(copy)
        return copy

    locals_ = [0]

    def local(src, dst):
        copy = pltpu.make_async_copy(src, dst, local_sem.at[locals_[0]])
        locals_[0] += 1
        copy.start()
        return copy

    loads = [local(gate_w, w_gate), local(up_w, w_up), local(down_w, w_down)]

    barrier = pltpu.get_barrier_semaphore()
    for peer in peers:
        pl.semaphore_signal(barrier, inc=1, device_id=peer, device_id_type=MESH)
    pl.semaphore_wait(barrier, len(peers))

    def block(yl_, z_, c_):
        return yl_ * 8 + z_ * 2 + c_

    def rows(b, part=0, size=128):
        return aligned(b * 128 + part * 64, size, 64)

    def gather_row(own, whole):
        me = block(yl, z, c)
        spot = whole.at[rows(me)]
        to_y = send(own, spot, yn)
        own_p, own_m = send(own, spot, zp), send(own, spot, zm)
        cores = [send(own, spot, co)]
        whole[rows(me), :] = own[...]
        yield
        to_y.wait_recv()
        spot = whole.at[rows(block(1 - yl, z, c))]
        mate_p, mate_m = send(spot, spot, zp), send(spot, spot, zm)
        cores.append(send(spot, spot, co))
        halves = []
        for y_, from_m, from_p in ((yl, own_p, own_m), (1 - yl, mate_p, mate_m)):
            from_m.wait_recv()
            b = block(y_, (z + 3) % 4, c)
            spot = whole.at[rows(b, 0, 64)]
            first = send(spot, spot, zp)
            spot = whole.at[rows(b)]
            cores.append(send(spot, spot, co))
            from_p.wait_recv()
            b = block(y_, (z + 1) % 4, c)
            spot = whole.at[rows(b, 1, 64)]
            second = send(spot, spot, zm)
            spot = whole.at[rows(b)]
            cores.append(send(spot, spot, co))
            halves.append((y_, first, second))
        yield
        for y_, first, second in halves:
            first.wait_recv()
            second.wait_recv()
            spot = whole.at[rows(block(y_, (z + 2) % 4, c))]
            cores.append(send(spot, spot, co))
        for copy in cores:
            copy.wait_recv()
        yield

    tok_steps = gather_row(tok, tok_all)
    cot_steps = gather_row(cot, cot_all)
    next(tok_steps)

    for copy in loads:
        copy.wait()
    @pl.loop(0, 8)
    def _(i):
        at = aligned(i * 128, 128)
        for j in range(7):
            cols = slice(j * 128, j * 128 + 128)
            kept_in = keep_in[i, j].astype(F32)
            w_gate[at, cols] = (w_gate[at, cols].astype(F32) * kept_in).astype(BF)
            w_up[at, cols] = (w_up[at, cols].astype(F32) * kept_in).astype(BF)

    @pl.loop(0, 7)
    def _(i):
        at = aligned(i * 128, 128)
        for j in range(8):
            cols = slice(j * 128, j * 128 + 128)
            kept_out = keep_out[i, j].astype(F32)
            w_down[at, cols] = (w_down[at, cols].astype(F32) * kept_out).astype(BF)

    next(tok_steps)
    next(cot_steps)
    next(tok_steps)
    flips = []

    def flip(first, last):
        for i in range(first, last):
            if len(flips) >= 2:
                flips[-2].wait()
            at = slice(i * 128, i * 128 + 128)
            tok_t[i % 2] = tok_all[:, at].T
            flips.append(local(tok_t.at[i % 2], tok_t_hbm.at[at]))

    downs = []

    def down_grad(i):
        if len(downs) >= 2:
            downs[-2].wait()
        units = slice(i * 128, i * 128 + 128)
        left = hid_all[:, units].T

        @pl.loop(0, 4)
        def _(t):
            v = jnp.dot(left, cot_all[:, aligned(t * 256, 256, 256)], preferred_element_type=F32)
            for j in range(2):
                kept_out = keep_out[i, 2 * t + j].astype(F32)
                down_t[i % 2, :, aligned(t * 256 + j * 128, 128)] = (
                    v[:, j * 128 : j * 128 + 128] * kept_out
                )
        downs.append(local(down_t.at[i % 2], down_hbm.at[units]))

    def tiles(body):
        @pl.loop(0, 3)
        def _(t):
            body(aligned(t * 256, 256, 256))

        body(pl.ds(768, 128))

    def product_of(lhs, rhs, transposed):
        def product(start, size, emit):
            at = aligned(start, size)

            def body(cols):
                if transposed:
                    v = lax.dot_general(
                        lhs[at, :], rhs[cols, :], (((1,), (1,)), ((), ())),
                        preferred_element_type=F32,
                    )
                else:
                    v = jnp.dot(lhs[at, :], rhs[:, cols], preferred_element_type=F32)
                emit(v, cols)
            tiles(body)
        return product

    gate_of = product_of(tok_all, w_gate, False)
    upper_of = product_of(tok_all, w_up, False)
    grad_of = product_of(cot_all, w_down, True)
    far, after, before = (x + 2) % 4, (x + 1) % 4, (x + 3) % 4

    def put(target, *terms):
        def emit(v, cols):
            for ref, at in terms:
                v = v + ref[at, cols].astype(F32)
            ref, at = target
            ref[at, cols] = v.astype(ref.dtype)
        return emit

    def reduce_x(product, s2, sp, sm, ia, ib, rp, rm, ys, yr, own):
        lo, hi, one = pl.ds(0, 256), pl.ds(256, 256), pl.ds(0, 256)
        product(far * 512, 256, put((s2, lo)))
        mid_a = send(s2.at[lo], ia, xp)
        product(far * 512 + 256, 256, put((s2, hi)))
        mid_b = send(s2.at[hi], ib, xm)
        yield
        product(after * 512 + 256, 256, put((sp, hi)))
        fin = [send(sp.at[hi], rp.at[hi], xp)]
        product(before * 512, 256, put((sm, lo)))
        fin.append(send(sm.at[lo], rm.at[lo], xm))
        yield
        mid_a.wait_recv()
        product(after * 512, 256, put((sp, lo), (ia, one)))
        fin.append(send(sp.at[lo], rp.at[lo], xp))
        mid_b.wait_recv()
        product(before * 512 + 256, 256, put((sm, hi), (ib, one)))
        fin.append(send(sm.at[hi], rm.at[hi], xm))
        yield
        for copy in fin:
            copy.wait_recv()

        def total(half, target):
            at = aligned(half * 256, 256, 256)
            product(x * 512 + half * 256, 256, put((target, one), (rp, at), (rm, at)))

        total(1 - h, ys)
        over = send(ys, yr, yh)
        total(h, own)
        yield
        over.wait_recv()
        yield

    def reduce_y(product, ys, yr, s2, sp, sm, ia, ib, rp, rm, own):
        chunks = (far, after, before, x)
        over = []
        lo, hi, one, two = pl.ds(0, 128), pl.ds(128, 128), pl.ds(0, 128), pl.ds(0, 256)

        def cross(k):
            at = pl.ds(k * 256, 256)
            product(chunks[k] * 512 + (1 - h) * 256, 256, put((ys, at)))
            over.append(send(ys.at[at], yr.at[at], yh))

        def mine(k, half):
            return chunks[k] * 512 + h * 256 + half * 128

        def came(k, half):
            return (yr, pl.ds(k * 256 + half * 128, 128))

        cross(0)
        yield
        for k in range(1, 4):
            cross(k)
        yield
        over[0].wait_recv()
        product(mine(0, 0), 256, put((s2, two), (yr, pl.ds(0, 256))))
        mid_a = send(s2.at[lo], ia, xp)
        mid_b = send(s2.at[hi], ib, xm)
        yield
        over[1].wait_recv()
        product(mine(1, 1), 128, put((sp, hi), came(1, 1)))
        fin = [send(sp.at[hi], rp.at[hi], xp)]
        yield
        over[2].wait_recv()
        product(mine(2, 0), 128, put((sm, lo), came(2, 0)))
        fin.append(send(sm.at[lo], rm.at[lo], xm))
        mid_a.wait_recv()
        product(mine(1, 0), 128, put((sp, lo), came(1, 0), (ia, one)))
        fin.append(send(sp.at[lo], rp.at[lo], xp))
        mid_b.wait_recv()
        product(mine(2, 1), 128, put((sm, hi), came(2, 1), (ib, one)))
        fin.append(send(sm.at[hi], rm.at[hi], xm))
        yield
        over[3].wait_recv()
        for copy in fin:
            copy.wait_recv()
        product(mine(3, 0), 256, put((own, two), (yr, pl.ds(768, 256)), (rp, two), (rm, two)))
        yield

    def spot_in(whole, x_, h_, part=0, size=256):
        return whole.at[aligned(x_ * 512 + h_ * 256 + part * 128, size)]

    def gather_y(own, whole, arrived=None):
        def came(x_, h_):
            if arrived is not None:
                arrived(x_, h_)

        spot = spot_in(whole, x, h)
        to_y = send(own, spot, yh)
        mine = local(own, spot)
        yield
        own_p, own_m = send(own, spot, xp), send(own, spot, xm)
        mine.wait()
        came(x, h)
        yield
        to_y.wait_recv()
        spot = spot_in(whole, x, 1 - h)
        mate_p, mate_m = send(spot, spot, xp), send(spot, spot, xm)
        came(x, 1 - h)
        yield
        halves = []
        for h_, from_m, from_p in ((h, own_p, own_m), (1 - h, mate_p, mate_m)):
            from_m.wait_recv()
            spot = spot_in(whole, before, h_, 0, 128)
            halves.append(send(spot, spot, xp))
            from_p.wait_recv()
            spot = spot_in(whole, after, h_, 1, 128)
            halves.append(send(spot, spot, xm))
            came(before, h_)
            came(after, h_)
            yield
        for i, h_ in enumerate((h, 1 - h)):
            halves[2 * i].wait_recv()
            halves[2 * i + 1].wait_recv()
            came(far, h_)
        yield

    def gather_x(own, whole):
        spot = spot_in(whole, x, h)
        own_p, own_m = send(own, spot, xp), send(own, spot, xm)
        mine = local(own, spot)
        yield
        over = [send(own, spot, yh)]
        yield
        own_p.wait_recv()
        spot = spot_in(whole, before, h, 0, 128)
        half_a = send(spot, spot, xp)
        spot = spot_in(whole, before, h)
        over.append(send(spot, spot, yh))
        own_m.wait_recv()
        spot = spot_in(whole, after, h, 1, 128)
        half_b = send(spot, spot, xm)
        spot = spot_in(whole, after, h)
        over.append(send(spot, spot, yh))
        yield
        half_a.wait_recv()
        half_b.wait_recv()
        spot = spot_in(whole, far, h)
        over.append(send(spot, spot, yh))
        yield
        for copy in over:
            copy.wait_recv()
        mine.wait()
        yield

    core = []

    def cross_core(x_, h_):
        pair = x_ * 2 + h_

        @pl.loop(0, 4)
        def _(t):
            cols = aligned(t * 256, 256, 256)
            c_s[pair, :, cols] = jnp.dot(
                hid_all[rows(pair * 2 + 1 - c), :], w_down[:, cols], preferred_element_type=F32
            )
        core.append(send(c_s.at[pair], c_r.at[pair], co))

    gate = reduce_x(gate_of, g_s2, g_sp, g_sm, g_ia, g_ib, g_rp, g_rm, g_ys, g_yr, g_own)
    upper = reduce_y(upper_of, u_ys, u_yr, u_s2, u_sp, u_sm, u_ia, u_ib, u_rp, u_rm, u_own)
    grad = reduce_x(grad_of, h_s2, h_sp, h_sm, h_ia, h_ib, h_rp, h_rm, h_ys, h_yr, h_own)
    next(gate)
    next(upper)
    next(gate)
    next(upper)
    next(cot_steps)
    flip(0, 2)
    next(cot_steps)
    next(upper)
    next(gate)
    next(upper)
    next(grad)
    next(grad)
    flip(2, 4)
    next(upper)
    flip(4, 6)
    next(gate)
    flip(6, 8)
    next(grad)
    next(upper)
    next(gate)

    @pl.loop(0, 16)
    def _(t):
        at = aligned(t * 16, 16, 16)
        gate_v = g_own[at, :] + g_yr[at, :].astype(F32)
        upper_v = u_own[at, :]
        sigma = 1.0 / (1.0 + jnp.exp(-gate_v))
        swish = gate_v * sigma
        hid_own[at, :] = (swish * upper_v).astype(BF)
        g_own[at, :] = upper_v * sigma * (1.0 + gate_v * (1.0 - sigma))
        u_own[at, :] = swish

    hid = gather_y(hid_own, hid_all, cross_core)
    next(hid)
    next(hid)
    next(grad)
    next(hid)
    next(hid)
    next(grad)

    @pl.loop(0, 16)
    def _(t):
        at = aligned(t * 16, 16, 16)
        grad_v = h_own[at, :] + h_yr[at, :].astype(F32)
        gp_own[at, :] = (grad_v * g_own[at, :]).astype(BF)
        up_own[at, :] = (grad_v * u_own[at, :]).astype(BF)

    gp = gather_x(gp_own, gp_hbm)
    up = gather_y(up_own, up_hbm)
    next(up)
    next(gp)
    next(gp)
    next(hid)
    next(up)
    next(hid)
    next(up)
    next(gp)

    def kept(yl_, z_):
        def piece(cols):
            part = jnp.dot(
                hid_all[rows(block(yl_, z_, c)), :], w_down[:, cols], preferred_element_type=F32
            )
            return part + c_r[yl_ * 4 + z_, :, cols]
        return piece

    def over_cols(body):
        @pl.loop(0, 4)
        def _(t):
            body(aligned(t * 256, 256, 256))

    down_grad(0)
    for copy in core:
        copy.wait_recv()
    z_far, z_after, z_before = (z + 2) % 4, (z + 1) % 4, (z + 3) % 4

    def ring_piece(y_, z_, target, inc=None):
        piece = kept(y_, z_)

        def body(cols):
            v = piece(cols)
            if inc is not None:
                v = v + inc[:, cols]
            target[:, cols] = v
        over_cols(body)

    ring_piece(0, z_far, z_s2.at[0])
    z_mid_a = send(z_s2.at[0], z_i.at[0], zp)
    ring_piece(1, z_far, z_s2.at[1])
    z_mid_b = send(z_s2.at[1], z_i.at[1], zm)
    ring_piece(1, z_after, z_sp.at[1])
    z_fin = [send(z_sp.at[1], z_rp.at[1], zp)]
    ring_piece(0, z_before, z_sm.at[0])
    z_fin.append(send(z_sm.at[0], z_rm.at[0], zm))
    next(up)
    next(gp)
    down_grad(1)
    down_grad(2)
    z_mid_a.wait_recv()
    ring_piece(0, z_after, z_sp.at[0], z_i.at[0])
    z_fin.append(send(z_sp.at[0], z_rp.at[0], zp))
    z_mid_b.wait_recv()
    ring_piece(1, z_before, z_sm.at[1], z_i.at[1])
    z_fin.append(send(z_sm.at[1], z_rm.at[1], zm))
    down_grad(3)
    down_grad(4)
    next(up)
    down_grad(5)
    down_grad(6)
    for copy in z_fin:
        copy.wait_recv()

    def row_total(y_, target):
        piece = kept(y_, z)

        def body(cols):
            target[:, cols] = piece(cols) + z_rp[y_, :, cols] + z_rm[y_, :, cols]
        over_cols(body)

    row_total(1 - yl, o_ys)
    o_over = send(o_ys, o_yr, yn)
    row_total(yl, o_own)
    o_over.wait_recv()
    out[...] = (o_own[...] + o_yr[...]).astype(BF)
    next(up)
    next(gp)
    for copy in flips[-2:] + downs[-2:]:
        copy.wait()
    for copy in sent:
        copy.wait_send()


def forward(tokens, cotangent, gate_weight, up_weight, down_weight, keep_in, keep_out):
    hbm = pl.BlockSpec(memory_space=pl.ANY)
    vmem = pl.BlockSpec(memory_space=pltpu.VMEM)

    def bf(*shape):
        return pltpu.VMEM(shape, BF)

    def f32(*shape):
        return pltpu.VMEM(shape, F32)

    def ring(n):
        return [bf(n, 896)] * 3 + [bf(n // 2, 896)] * 2 + [bf(n, 896)] * 2

    def ring_y():
        return ring(512) + [bf(256, 896), bf(256, 896), f32(256, 896)]

    smem = pl.BlockSpec(memory_space=pltpu.SMEM)
    sds = jax.ShapeDtypeStruct
    return pl.pallas_call(
        forward_kernel,
        out_shape=(
            sds((128, 1024), BF), sds((1024, 2048), BF), sds((896, 1024), F32),
            sds((2048, 896), BF), sds((2048, 896), BF),
        ),
        in_specs=[vmem, vmem, hbm, hbm, hbm, smem, smem],
        out_specs=[vmem, hbm, hbm, hbm, hbm],
        scratch_shapes=[bf(1024, 896), bf(1024, 896), bf(896, 1024), bf(2048, 1024), bf(2048, 1024)]
        + ring_y()
        + ring_y()
        + [bf(1024, 896), bf(1024, 896)] + ring(256) + [f32(256, 896)]
        + [bf(256, 896)] * 3 + [bf(2048, 896)]
        + [f32(8, 128, 1024), f32(8, 128, 1024)]
        + [f32(2, 128, 1024)] * 6
        + [f32(128, 1024)] * 3
        + [bf(2, 128, 2048), f32(2, 128, 1024)]
        + [
            pltpu.SemaphoreType.DMA((SLOTS,)), pltpu.SemaphoreType.DMA((SLOTS,)),
            pltpu.SemaphoreType.DMA((24,)),
        ],
        compiler_params=pltpu.CompilerParams(
            collective_id=0, has_side_effects=True, vmem_limit_bytes=VMEM_LIMIT
        ),
    )(tokens, cotangent, gate_weight, up_weight, down_weight, keep_in, keep_out)


def input_grads_kernel(keep_in, tok_t, gp_hbm, up_hbm, gate_out, up_out, gp, up, sems):
    i = pl.program_id(0)
    gp_load = pltpu.make_async_copy(gp_hbm, gp, sems.at[0])
    up_load = pltpu.make_async_copy(up_hbm, up, sems.at[1])

    @pl.when(i == 0)
    def _():
        gp_load.start()
        up_load.start()
        gp_load.wait()

    def one(grads, target):
        def tile(cols, blocks, first):
            v = jnp.dot(tok_t[...], grads[:, cols], preferred_element_type=F32)
            for a in range(2):
                for b in range(blocks):
                    kept_in = keep_in[2 * i + a, first + b].astype(F32)
                    at = slice(a * 128, a * 128 + 128)
                    target[at, (first + b) * 128 : (first + b) * 128 + 128] = (
                        v[at, b * 128 : b * 128 + 128] * kept_in
                    )
        for t in range(3):
            tile(slice(t * 256, t * 256 + 256), 2, 2 * t)
        tile(slice(768, 896), 1, 6)

    one(gp, gate_out)

    @pl.when(i == 0)
    def _():
        up_load.wait()

    one(up, up_out)


def input_grads(keep_in, tok_t, gp, up):
    whole = pl.BlockSpec(memory_space=pl.ANY)
    piece = pl.BlockSpec((256, 896), lambda i: (i, 0))
    return pl.pallas_call(
        input_grads_kernel,
        grid=(4,),
        out_shape=(jax.ShapeDtypeStruct((1024, 896), F32),) * 2,
        in_specs=[
            pl.BlockSpec(memory_space=pltpu.SMEM),
            pl.BlockSpec((256, 2048), lambda i: (i, 0)), whole, whole,
        ],
        out_specs=[piece, piece],
        scratch_shapes=[
            pltpu.VMEM((2048, 896), BF), pltpu.VMEM((2048, 896), BF), pltpu.SemaphoreType.DMA((2,)),
        ],
        compiler_params=pltpu.CompilerParams(vmem_limit_bytes=VMEM_LIMIT),
        cost_estimate=pl.CostEstimate(
            flops=4 * 2048 * 1024 * 896, bytes_accessed=20 * 2**20, transcendentals=0
        ),
    )(keep_in, tok_t, gp, up)


def shards(tokens, gate_weight, up_weight, down_weight, input_mask, output_mask, cotangent):
    output, tok_t, grad_down, gp, up = forward(
        tokens, cotangent, gate_weight, up_weight, down_weight, input_mask, output_mask
    )
    grad_gate, grad_up = input_grads(input_mask, tok_t, gp, up)
    return (output, grad_gate, grad_up, grad_down)


def solution(mesh):
    placed = (
        P("row", "col"), P("col", "row"), P("col", "row"), P("row", "col"),
        P("col", "row"), P("row", "col"), P("row", "col"),
    )
    return jax.shard_map(
        shards, mesh=mesh, in_specs=placed,
        out_specs=(P("row", "col"), P("col", "row"), P("col", "row"), P("row", "col")),
        check_vma=False,
    )
```

```python
import jax
import jax.numpy as jnp
from jax import lax
from jax.experimental import pallas as pl
from jax.experimental.pallas import tpu as pltpu
from jax.sharding import PartitionSpec as P

BF = jnp.bfloat16
F32 = jnp.float32
MESH = pl.DeviceIdType.MESH
VMEM_LIMIT = 62 * 2**20
SLOTS = 112


def aligned(start, size, to=128):
    return pl.ds(pl.multiple_of(start, to), size)


def forward_kernel(
    tok, cot, gate_w, up_w, down_w, keep_in, keep_out,
    out, tok_t_hbm, down_hbm, gp_hbm, up_hbm,
    w_gate, w_up, w_down, tok_all, cot_all,
    g_s2, g_sp, g_sm, g_ia, g_ib, g_rp, g_rm, g_ys, g_yr, g_own,
    h_s2, h_sp, h_sm, h_ia, h_ib, h_rp, h_rm, h_ys, h_yr, h_own,
    u_ys, u_yr, u_s2, u_sp, u_sm, u_ia, u_ib, u_rp, u_rm, u_own,
    hid_own, gp_own, up_own, hid_all,
    c_s, c_r, z_s2, z_i, z_sp, z_sm, z_rp, z_rm, o_ys, o_yr, o_own, tok_t, down_t,
    send_sem, recv_sem, local_sem,
):
    row = lax.axis_index("row")
    col = lax.axis_index("col")
    x, h = col // 2, col % 2
    yl, z, c = row // 8, (row // 2) % 4, row % 2

    def device(x_, h_, yl_, z_, c_):
        return (yl_ * 8 + z_ * 2 + c_, x_ * 2 + h_)

    xp = device((x + 1) % 4, h, yl, z, c)
    xm = device((x + 3) % 4, h, yl, z, c)
    yh = device(x, 1 - h, yl, z, c)
    yn = device(x, h, 1 - yl, z, c)
    zp = device(x, h, yl, (z + 1) % 4, c)
    zm = device(x, h, yl, (z + 3) % 4, c)
    co = device(x, h, yl, z, 1 - c)
    peers = (xp, xm, yh, yn, zp, zm, co)

    slot = [0]
    sent = []

    def send(src, dst, peer):
        i = slot[0]
        slot[0] += 1
        copy = pltpu.make_async_remote_copy(
            src_ref=src, dst_ref=dst, send_sem=send_sem.at[i], recv_sem=recv_sem.at[i],
            device_id=peer, device_id_type=MESH,
        )
        copy.start()
        sent.append(copy)
        return copy

    locals_ = [0]

    def local(src, dst):
        copy = pltpu.make_async_copy(src, dst, local_sem.at[locals_[0]])
        locals_[0] += 1
        copy.start()
        return copy

    loads = [local(gate_w, w_gate), local(up_w, w_up), local(down_w, w_down)]

    barrier = pltpu.get_barrier_semaphore()
    for peer in peers:
        pl.semaphore_signal(barrier, inc=1, device_id=peer, device_id_type=MESH)
    pl.semaphore_wait(barrier, len(peers))

    def block(yl_, z_, c_):
        return yl_ * 8 + z_ * 2 + c_

    def rows(b, part=0, size=128):
        return aligned(b * 128 + part * 64, size, 64)

    def gather_row(own, whole):
        me = block(yl, z, c)
        spot = whole.at[rows(me)]
        to_y = send(own, spot, yn)
        own_p, own_m = send(own, spot, zp), send(own, spot, zm)
        cores = [send(own, spot, co)]
        whole[rows(me), :] = own[...]
        yield
        to_y.wait_recv()
        spot = whole.at[rows(block(1 - yl, z, c))]
        mate_p, mate_m = send(spot, spot, zp), send(spot, spot, zm)
        cores.append(send(spot, spot, co))
        halves = []
        for y_, from_m, from_p in ((yl, own_p, own_m), (1 - yl, mate_p, mate_m)):
            from_m.wait_recv()
            b = block(y_, (z + 3) % 4, c)
            spot = whole.at[rows(b, 0, 64)]
            first = send(spot, spot, zp)
            spot = whole.at[rows(b)]
            cores.append(send(spot, spot, co))
            from_p.wait_recv()
            b = block(y_, (z + 1) % 4, c)
            spot = whole.at[rows(b, 1, 64)]
            second = send(spot, spot, zm)
            spot = whole.at[rows(b)]
            cores.append(send(spot, spot, co))
            halves.append((y_, first, second))
        yield
        for y_, first, second in halves:
            first.wait_recv()
            second.wait_recv()
            spot = whole.at[rows(block(y_, (z + 2) % 4, c))]
            cores.append(send(spot, spot, co))
        for copy in cores:
            copy.wait_recv()
        yield

    tok_steps = gather_row(tok, tok_all)
    cot_steps = gather_row(cot, cot_all)
    next(tok_steps)

    for copy in loads:
        copy.wait()
    @pl.loop(0, 8)
    def _(i):
        at = aligned(i * 128, 128)
        for j in range(7):
            cols = slice(j * 128, j * 128 + 128)
            kept_in = keep_in[i, j].astype(F32)
            w_gate[at, cols] = (w_gate[at, cols].astype(F32) * kept_in).astype(BF)
            w_up[at, cols] = (w_up[at, cols].astype(F32) * kept_in).astype(BF)

    @pl.loop(0, 7)
    def _(i):
        at = aligned(i * 128, 128)
        for j in range(8):
            cols = slice(j * 128, j * 128 + 128)
            kept_out = keep_out[i, j].astype(F32)
            w_down[at, cols] = (w_down[at, cols].astype(F32) * kept_out).astype(BF)

    next(tok_steps)
    next(cot_steps)
    next(tok_steps)
    flips = []

    def flip(first, last):
        for i in range(first, last):
            if len(flips) >= 2:
                flips[-2].wait()
            at = slice(i * 128, i * 128 + 128)
            tok_t[i % 2] = tok_all[:, at].T
            flips.append(local(tok_t.at[i % 2], tok_t_hbm.at[at]))

    downs = []

    def down_grad(i):
        if len(downs) >= 2:
            downs[-2].wait()
        units = slice(i * 128, i * 128 + 128)
        left = hid_all[:, units].T

        @pl.loop(0, 4)
        def _(t):
            v = jnp.dot(left, cot_all[:, aligned(t * 256, 256, 256)], preferred_element_type=F32)
            for j in range(2):
                kept_out = keep_out[i, 2 * t + j].astype(F32)
                down_t[i % 2, :, aligned(t * 256 + j * 128, 128)] = (
                    v[:, j * 128 : j * 128 + 128] * kept_out
                )
        downs.append(local(down_t.at[i % 2], down_hbm.at[units]))

    def tiles(body):
        @pl.loop(0, 3)
        def _(t):
            body(aligned(t * 256, 256, 256))

        body(pl.ds(768, 128))

    def product_of(lhs, rhs, transposed):
        def product(start, size, emit):
            at = aligned(start, size)

            def body(cols):
                if transposed:
                    v = lax.dot_general(
                        lhs[at, :], rhs[cols, :], (((1,), (1,)), ((), ())),
                        preferred_element_type=F32,
                    )
                else:
                    v = jnp.dot(lhs[at, :], rhs[:, cols], preferred_element_type=F32)
                emit(v, cols)
            tiles(body)
        return product

    gate_of = product_of(tok_all, w_gate, False)
    upper_of = product_of(tok_all, w_up, False)
    grad_of = product_of(cot_all, w_down, True)
    far, after, before = (x + 2) % 4, (x + 1) % 4, (x + 3) % 4

    def put(target, *terms):
        def emit(v, cols):
            for ref, at in terms:
                v = v + ref[at, cols].astype(F32)
            ref, at = target
            ref[at, cols] = v.astype(ref.dtype)
        return emit

    def reduce_x(product, s2, sp, sm, ia, ib, rp, rm, ys, yr, own):
        lo, hi, one = pl.ds(0, 256), pl.ds(256, 256), pl.ds(0, 256)
        product(far * 512, 256, put((s2, lo)))
        mid_a = send(s2.at[lo], ia, xp)
        product(far * 512 + 256, 256, put((s2, hi)))
        mid_b = send(s2.at[hi], ib, xm)
        yield
        product(after * 512 + 256, 256, put((sp, hi)))
        fin = [send(sp.at[hi], rp.at[hi], xp)]
        product(before * 512, 256, put((sm, lo)))
        fin.append(send(sm.at[lo], rm.at[lo], xm))
        yield
        mid_a.wait_recv()
        product(after * 512, 256, put((sp, lo), (ia, one)))
        fin.append(send(sp.at[lo], rp.at[lo], xp))
        mid_b.wait_recv()
        product(before * 512 + 256, 256, put((sm, hi), (ib, one)))
        fin.append(send(sm.at[hi], rm.at[hi], xm))
        yield
        for copy in fin:
            copy.wait_recv()

        def total(half, target):
            at = aligned(half * 256, 256, 256)
            product(x * 512 + half * 256, 256, put((target, one), (rp, at), (rm, at)))

        total(1 - h, ys)
        over = send(ys, yr, yh)
        total(h, own)
        yield
        over.wait_recv()
        yield

    def reduce_y(product, ys, yr, s2, sp, sm, ia, ib, rp, rm, own):
        chunks = (far, after, before, x)
        over = []
        lo, hi, one, two = pl.ds(0, 128), pl.ds(128, 128), pl.ds(0, 128), pl.ds(0, 256)

        def cross(k):
            at = pl.ds(k * 256, 256)
            product(chunks[k] * 512 + (1 - h) * 256, 256, put((ys, at)))
            over.append(send(ys.at[at], yr.at[at], yh))

        def mine(k, half):
            return chunks[k] * 512 + h * 256 + half * 128

        def came(k, half):
            return (yr, pl.ds(k * 256 + half * 128, 128))

        cross(0)
        yield
        for k in range(1, 4):
            cross(k)
        yield
        over[0].wait_recv()
        product(mine(0, 0), 256, put((s2, two), (yr, pl.ds(0, 256))))
        mid_a = send(s2.at[lo], ia, xp)
        mid_b = send(s2.at[hi], ib, xm)
        yield
        over[1].wait_recv()
        product(mine(1, 1), 128, put((sp, hi), came(1, 1)))
        fin = [send(sp.at[hi], rp.at[hi], xp)]
        yield
        over[2].wait_recv()
        product(mine(2, 0), 128, put((sm, lo), came(2, 0)))
        fin.append(send(sm.at[lo], rm.at[lo], xm))
        mid_a.wait_recv()
        product(mine(1, 0), 128, put((sp, lo), came(1, 0), (ia, one)))
        fin.append(send(sp.at[lo], rp.at[lo], xp))
        mid_b.wait_recv()
        product(mine(2, 1), 128, put((sm, hi), came(2, 1), (ib, one)))
        fin.append(send(sm.at[hi], rm.at[hi], xm))
        yield
        over[3].wait_recv()
        for copy in fin:
            copy.wait_recv()
        product(mine(3, 0), 256, put((own, two), (yr, pl.ds(768, 256)), (rp, two), (rm, two)))
        yield

    def spot_in(whole, x_, h_, part=0, size=256):
        return whole.at[aligned(x_ * 512 + h_ * 256 + part * 128, size)]

    def gather_y(own, whole, arrived=None):
        def came(x_, h_):
            if arrived is not None:
                arrived(x_, h_)

        spot = spot_in(whole, x, h)
        to_y = send(own, spot, yh)
        mine = local(own, spot)
        yield
        own_p, own_m = send(own, spot, xp), send(own, spot, xm)
        mine.wait()
        came(x, h)
        yield
        to_y.wait_recv()
        spot = spot_in(whole, x, 1 - h)
        mate_p, mate_m = send(spot, spot, xp), send(spot, spot, xm)
        came(x, 1 - h)
        yield
        halves = []
        for h_, from_m, from_p in ((h, own_p, own_m), (1 - h, mate_p, mate_m)):
            from_m.wait_recv()
            spot = spot_in(whole, before, h_, 0, 128)
            halves.append(send(spot, spot, xp))
            from_p.wait_recv()
            spot = spot_in(whole, after, h_, 1, 128)
            halves.append(send(spot, spot, xm))
            came(before, h_)
            came(after, h_)
            yield
        for i, h_ in enumerate((h, 1 - h)):
            halves[2 * i].wait_recv()
            halves[2 * i + 1].wait_recv()
            came(far, h_)
        yield

    def gather_x(own, whole):
        spot = spot_in(whole, x, h)
        own_p, own_m = send(own, spot, xp), send(own, spot, xm)
        mine = local(own, spot)
        yield
        over = [send(own, spot, yh)]
        yield
        own_p.wait_recv()
        spot = spot_in(whole, before, h, 0, 128)
        half_a = send(spot, spot, xp)
        spot = spot_in(whole, before, h)
        over.append(send(spot, spot, yh))
        own_m.wait_recv()
        spot = spot_in(whole, after, h, 1, 128)
        half_b = send(spot, spot, xm)
        spot = spot_in(whole, after, h)
        over.append(send(spot, spot, yh))
        yield
        half_a.wait_recv()
        half_b.wait_recv()
        spot = spot_in(whole, far, h)
        over.append(send(spot, spot, yh))
        yield
        for copy in over:
            copy.wait_recv()
        mine.wait()
        yield

    core = []

    def cross_core(x_, h_):
        pair = x_ * 2 + h_

        @pl.loop(0, 4)
        def _(t):
            cols = aligned(t * 256, 256, 256)
            c_s[pair, :, cols] = jnp.dot(
                hid_all[rows(pair * 2 + 1 - c), :], w_down[:, cols], preferred_element_type=F32
            )
        core.append(send(c_s.at[pair], c_r.at[pair], co))

    gate = reduce_x(gate_of, g_s2, g_sp, g_sm, g_ia, g_ib, g_rp, g_rm, g_ys, g_yr, g_own)
    upper = reduce_y(upper_of, u_ys, u_yr, u_s2, u_sp, u_sm, u_ia, u_ib, u_rp, u_rm, u_own)
    grad = reduce_x(grad_of, h_s2, h_sp, h_sm, h_ia, h_ib, h_rp, h_rm, h_ys, h_yr, h_own)
    next(gate)
    next(upper)
    next(gate)
    next(upper)
    next(cot_steps)
    flip(0, 2)
    next(cot_steps)
    next(upper)
    next(gate)
    next(upper)
    next(grad)
    next(grad)
    flip(2, 4)
    next(upper)
    flip(4, 6)
    next(gate)
    flip(6, 8)
    next(grad)
    next(upper)
    next(gate)

    @pl.loop(0, 16)
    def _(t):
        at = aligned(t * 16, 16, 16)
        gate_v = g_own[at, :] + g_yr[at, :].astype(F32)
        upper_v = u_own[at, :]
        sigma = 1.0 / (1.0 + jnp.exp(-gate_v))
        swish = gate_v * sigma
        hid_own[at, :] = (swish * upper_v).astype(BF)
        g_own[at, :] = upper_v * sigma * (1.0 + gate_v * (1.0 - sigma))
        u_own[at, :] = swish

    hid = gather_y(hid_own, hid_all, cross_core)
    next(hid)
    next(hid)
    next(grad)
    next(hid)
    next(hid)
    next(grad)

    @pl.loop(0, 16)
    def _(t):
        at = aligned(t * 16, 16, 16)
        grad_v = h_own[at, :] + h_yr[at, :].astype(F32)
        gp_own[at, :] = (grad_v * g_own[at, :]).astype(BF)
        up_own[at, :] = (grad_v * u_own[at, :]).astype(BF)

    gp = gather_x(gp_own, gp_hbm)
    up = gather_y(up_own, up_hbm)
    next(up)
    next(gp)
    next(gp)
    next(hid)
    next(up)
    next(hid)
    next(up)
    next(gp)

    def kept(yl_, z_):
        def piece(cols):
            part = jnp.dot(
                hid_all[rows(block(yl_, z_, c)), :], w_down[:, cols], preferred_element_type=F32
            )
            return part + c_r[yl_ * 4 + z_, :, cols]
        return piece

    def over_cols(body):
        @pl.loop(0, 4)
        def _(t):
            body(aligned(t * 256, 256, 256))

    down_grad(0)
    for copy in core:
        copy.wait_recv()
    z_far, z_after, z_before = (z + 2) % 4, (z + 1) % 4, (z + 3) % 4

    def ring_piece(y_, z_, target, inc=None):
        piece = kept(y_, z_)

        def body(cols):
            v = piece(cols)
            if inc is not None:
                v = v + inc[:, cols]
            target[:, cols] = v
        over_cols(body)

    ring_piece(0, z_far, z_s2.at[0])
    z_mid_a = send(z_s2.at[0], z_i.at[0], zp)
    ring_piece(1, z_far, z_s2.at[1])
    z_mid_b = send(z_s2.at[1], z_i.at[1], zm)
    ring_piece(1, z_after, z_sp.at[1])
    z_fin = [send(z_sp.at[1], z_rp.at[1], zp)]
    ring_piece(0, z_before, z_sm.at[0])
    z_fin.append(send(z_sm.at[0], z_rm.at[0], zm))
    next(up)
    next(gp)
    down_grad(1)
    down_grad(2)
    z_mid_a.wait_recv()
    ring_piece(0, z_after, z_sp.at[0], z_i.at[0])
    z_fin.append(send(z_sp.at[0], z_rp.at[0], zp))
    z_mid_b.wait_recv()
    ring_piece(1, z_before, z_sm.at[1], z_i.at[1])
    z_fin.append(send(z_sm.at[1], z_rm.at[1], zm))
    down_grad(3)
    down_grad(4)
    next(up)
    down_grad(5)
    down_grad(6)
    for copy in z_fin:
        copy.wait_recv()

    def row_total(y_, target):
        piece = kept(y_, z)

        def body(cols):
            target[:, cols] = piece(cols) + z_rp[y_, :, cols] + z_rm[y_, :, cols]
        over_cols(body)

    row_total(1 - yl, o_ys)
    o_over = send(o_ys, o_yr, yn)
    row_total(yl, o_own)
    o_over.wait_recv()
    out[...] = (o_own[...] + o_yr[...]).astype(BF)
    next(up)
    next(gp)
    for copy in flips[-2:] + downs[-2:]:
        copy.wait()
    for copy in sent:
        copy.wait_send()


def forward(tokens, cotangent, gate_weight, up_weight, down_weight, keep_in, keep_out):
    hbm = pl.BlockSpec(memory_space=pl.ANY)
    vmem = pl.BlockSpec(memory_space=pltpu.VMEM)

    def bf(*shape):
        return pltpu.VMEM(shape, BF)

    def f32(*shape):
        return pltpu.VMEM(shape, F32)

    def ring(n):
        return [bf(n, 896)] * 3 + [bf(n // 2, 896)] * 2 + [bf(n, 896)] * 2

    def ring_y():
        return ring(512) + [bf(256, 896), bf(256, 896), f32(256, 896)]

    smem = pl.BlockSpec(memory_space=pltpu.SMEM)
    sds = jax.ShapeDtypeStruct
    return pl.pallas_call(
        forward_kernel,
        out_shape=(
            sds((128, 1024), BF), sds((1024, 2048), BF), sds((896, 1024), F32),
            sds((2048, 896), BF), sds((2048, 896), BF),
        ),
        in_specs=[vmem, vmem, hbm, hbm, hbm, smem, smem],
        out_specs=[vmem, hbm, hbm, hbm, hbm],
        scratch_shapes=[bf(1024, 896), bf(1024, 896), bf(896, 1024), bf(2048, 1024), bf(2048, 1024)]
        + ring_y()
        + ring_y()
        + [bf(1024, 896), bf(1024, 896)] + ring(256) + [f32(256, 896)]
        + [bf(256, 896)] * 3 + [bf(2048, 896)]
        + [f32(8, 128, 1024), f32(8, 128, 1024)]
        + [f32(2, 128, 1024)] * 6
        + [f32(128, 1024)] * 3
        + [bf(2, 128, 2048), f32(2, 128, 1024)]
        + [
            pltpu.SemaphoreType.DMA((SLOTS,)), pltpu.SemaphoreType.DMA((SLOTS,)),
            pltpu.SemaphoreType.DMA((24,)),
        ],
        compiler_params=pltpu.CompilerParams(
            collective_id=0, has_side_effects=True, vmem_limit_bytes=VMEM_LIMIT
        ),
    )(tokens, cotangent, gate_weight, up_weight, down_weight, keep_in, keep_out)


def input_grads_kernel(
    keep_in, tok_t_hbm, gp_hbm, up_hbm, down_hbm, out_hbm,
    gate_grad, up_grad, down_grad, output, tok_t, gp, up, down, out, done, sems,
):
    lo, hi = slice(0, 512), slice(512, 1024)
    moves = (
        (tok_t_hbm.at[lo], tok_t.at[lo]), (gp_hbm, gp), (up_hbm, up),
        (tok_t_hbm.at[hi], tok_t.at[hi]), (down_hbm, down), (out_hbm, out),
    )
    loads = [pltpu.make_async_copy(src, dst, sems.at[i]) for i, (src, dst) in enumerate(moves)]
    for load in loads:
        load.start()
    stores = []

    def part(half, grads, target):
        k = len(stores)
        if k >= 2:
            stores[k - 2].wait()
        at = slice(half * 512, half * 512 + 512)
        buf = done.at[k % 2]

        def tile(start, first, blocks):
            v = jnp.dot(
                tok_t[at, :], grads[:, aligned(start, blocks * 128)], preferred_element_type=F32
            )
            for i in range(4):
                for j in range(blocks):
                    kept_in = keep_in[half * 4 + i, first + j].astype(F32)
                    buf[i * 128 : i * 128 + 128, aligned(start + j * 128, 128)] = (
                        v[i * 128 : i * 128 + 128, j * 128 : j * 128 + 128] * kept_in
                    )

        @pl.loop(0, 3)
        def _(t):
            tile(t * 256, 2 * t, 2)

        tile(768, 6, 1)
        store = pltpu.make_async_copy(buf, target.at[at], sems.at[6 + k])
        store.start()
        stores.append(store)

    loads[0].wait()
    loads[1].wait()
    part(0, gp, gate_grad)
    loads[2].wait()
    part(0, up, up_grad)
    loads[3].wait()
    loads[4].wait()
    loads[5].wait()
    passed = [
        pltpu.make_async_copy(down, down_grad, sems.at[10]),
        pltpu.make_async_copy(out, output, sems.at[11]),
    ]
    for copy in passed:
        copy.start()
    part(1, gp, gate_grad)
    part(1, up, up_grad)
    for copy in passed + stores[2:]:
        copy.wait()


def input_grads(keep_in, tok_t, gp, up, down, out):
    hbm = pl.BlockSpec(memory_space=pl.ANY)
    sds = jax.ShapeDtypeStruct
    return pl.pallas_call(
        input_grads_kernel,
        out_shape=(
            sds((1024, 896), F32), sds((1024, 896), F32), sds((896, 1024), F32),
            sds((128, 1024), BF),
        ),
        in_specs=[pl.BlockSpec(memory_space=pltpu.SMEM)] + [hbm] * 5,
        out_specs=[hbm] * 4,
        scratch_shapes=[
            pltpu.VMEM((1024, 2048), BF), pltpu.VMEM((2048, 896), BF),
            pltpu.VMEM((2048, 896), BF), pltpu.VMEM((896, 1024), F32),
            pltpu.VMEM((128, 1024), BF), pltpu.VMEM((2, 512, 896), F32),
            pltpu.SemaphoreType.DMA((12,)),
        ],
        compiler_params=pltpu.CompilerParams(vmem_limit_bytes=VMEM_LIMIT),
    )(keep_in, tok_t, gp, up, down, out)


def shards(tokens, gate_weight, up_weight, down_weight, input_mask, output_mask, cotangent):
    out, tok_t, down, gp, up = forward(
        tokens, cotangent, gate_weight, up_weight, down_weight, input_mask, output_mask
    )
    grad_gate, grad_up, grad_down, output = input_grads(input_mask, tok_t, gp, up, down, out)
    return (output, grad_gate, grad_up, grad_down)


def solution(mesh):
    placed = (
        P("row", "col"), P("col", "row"), P("col", "row"), P("row", "col"),
        P("col", "row"), P("row", "col"), P("row", "col"),
    )
    return jax.shard_map(
        shards, mesh=mesh, in_specs=placed,
        out_specs=(P("row", "col"), P("col", "row"), P("col", "row"), P("row", "col")),
        check_vma=False,
    )
```

```python
import jax
import jax.numpy as jnp
from jax import lax
from jax.experimental import pallas as pl
from jax.experimental.pallas import tpu as pltpu
from jax.sharding import PartitionSpec as P

BF = jnp.bfloat16
F32 = jnp.float32
MESH = pl.DeviceIdType.MESH
VMEM_LIMIT = 62 * 2**20
SLOTS = 112
K2_ROWS = 256


def aligned(start, size, to=128):
    return pl.ds(pl.multiple_of(start, to), size)


def forward_kernel(
    tok, cot, gate_w, up_w, down_w, keep_in, keep_out,
    out, tok_t_hbm, down_hbm, gp_hbm, up_hbm,
    w_gate, w_up, w_down, tok_all, cot_all,
    g_s2, g_sp, g_sm, g_ia, g_ib, g_rp, g_rm, g_ys, g_yr, g_own,
    h_s2, h_sp, h_sm, h_ia, h_ib, h_rp, h_rm, h_ys, h_yr, h_own,
    u_ys, u_yr, u_s2, u_sp, u_sm, u_ia, u_ib, u_rp, u_rm, u_own,
    hid_own, gp_own, up_own, hid_all,
    c_s, c_r, z_s2, z_i, z_sp, z_sm, z_rp, z_rm, o_ys, o_yr, o_own, tok_t, down_t,
    send_sem, recv_sem, local_sem,
):
    row = lax.axis_index("row")
    col = lax.axis_index("col")
    x, h = col // 2, col % 2
    yl, z, c = row // 8, (row // 2) % 4, row % 2

    def device(x_, h_, yl_, z_, c_):
        return (yl_ * 8 + z_ * 2 + c_, x_ * 2 + h_)

    xp = device((x + 1) % 4, h, yl, z, c)
    xm = device((x + 3) % 4, h, yl, z, c)
    yh = device(x, 1 - h, yl, z, c)
    yn = device(x, h, 1 - yl, z, c)
    zp = device(x, h, yl, (z + 1) % 4, c)
    zm = device(x, h, yl, (z + 3) % 4, c)
    co = device(x, h, yl, z, 1 - c)
    peers = (xp, xm, yh, yn, zp, zm, co)

    slot = [0]
    sent = []

    def send(src, dst, peer):
        i = slot[0]
        slot[0] += 1
        copy = pltpu.make_async_remote_copy(
            src_ref=src, dst_ref=dst, send_sem=send_sem.at[i], recv_sem=recv_sem.at[i],
            device_id=peer, device_id_type=MESH,
        )
        copy.start()
        sent.append(copy)
        return copy

    locals_ = [0]

    def local(src, dst):
        copy = pltpu.make_async_copy(src, dst, local_sem.at[locals_[0]])
        locals_[0] += 1
        copy.start()
        return copy

    loads = [local(gate_w, w_gate), local(up_w, w_up), local(down_w, w_down)]

    barrier = pltpu.get_barrier_semaphore()
    for peer in peers:
        pl.semaphore_signal(barrier, inc=1, device_id=peer, device_id_type=MESH)
    pl.semaphore_wait(barrier, len(peers))

    def block(yl_, z_, c_):
        return yl_ * 8 + z_ * 2 + c_

    def rows(b, part=0, size=128):
        return aligned(b * 128 + part * 64, size, 64)

    def gather_row(own, whole):
        me = block(yl, z, c)
        spot = whole.at[rows(me)]
        to_y = send(own, spot, yn)
        own_p, own_m = send(own, spot, zp), send(own, spot, zm)
        cores = [send(own, spot, co)]
        whole[rows(me), :] = own[...]
        yield
        to_y.wait_recv()
        spot = whole.at[rows(block(1 - yl, z, c))]
        mate_p, mate_m = send(spot, spot, zp), send(spot, spot, zm)
        cores.append(send(spot, spot, co))
        halves = []
        for y_, from_m, from_p in ((yl, own_p, own_m), (1 - yl, mate_p, mate_m)):
            from_m.wait_recv()
            b = block(y_, (z + 3) % 4, c)
            spot = whole.at[rows(b, 0, 64)]
            first = send(spot, spot, zp)
            spot = whole.at[rows(b)]
            cores.append(send(spot, spot, co))
            from_p.wait_recv()
            b = block(y_, (z + 1) % 4, c)
            spot = whole.at[rows(b, 1, 64)]
            second = send(spot, spot, zm)
            spot = whole.at[rows(b)]
            cores.append(send(spot, spot, co))
            halves.append((y_, first, second))
        yield
        for y_, first, second in halves:
            first.wait_recv()
            second.wait_recv()
            spot = whole.at[rows(block(y_, (z + 2) % 4, c))]
            cores.append(send(spot, spot, co))
        for copy in cores:
            copy.wait_recv()
        yield

    tok_steps = gather_row(tok, tok_all)
    cot_steps = gather_row(cot, cot_all)
    next(tok_steps)

    for copy in loads:
        copy.wait()
    @pl.loop(0, 8)
    def _(i):
        at = aligned(i * 128, 128)
        for j in range(7):
            cols = slice(j * 128, j * 128 + 128)
            kept_in = keep_in[i, j].astype(F32)
            w_gate[at, cols] = (w_gate[at, cols].astype(F32) * kept_in).astype(BF)
            w_up[at, cols] = (w_up[at, cols].astype(F32) * kept_in).astype(BF)

    @pl.loop(0, 7)
    def _(i):
        at = aligned(i * 128, 128)
        for j in range(8):
            cols = slice(j * 128, j * 128 + 128)
            kept_out = keep_out[i, j].astype(F32)
            w_down[at, cols] = (w_down[at, cols].astype(F32) * kept_out).astype(BF)

    next(tok_steps)
    next(cot_steps)
    next(tok_steps)
    flips = []

    def flip(first, last):
        for i in range(first, last):
            if len(flips) >= 2:
                flips[-2].wait()
            at = slice(i * 128, i * 128 + 128)
            tok_t[i % 2] = tok_all[:, at].T
            flips.append(local(tok_t.at[i % 2], tok_t_hbm.at[at]))

    downs = []

    def down_grad(i):
        if len(downs) >= 2:
            downs[-2].wait()
        units = slice(i * 128, i * 128 + 128)
        left = hid_all[:, units].T

        @pl.loop(0, 4)
        def _(t):
            v = jnp.dot(left, cot_all[:, aligned(t * 256, 256, 256)], preferred_element_type=F32)
            for j in range(2):
                kept_out = keep_out[i, 2 * t + j].astype(F32)
                down_t[i % 2, :, aligned(t * 256 + j * 128, 128)] = (
                    v[:, j * 128 : j * 128 + 128] * kept_out
                )
        downs.append(local(down_t.at[i % 2], down_hbm.at[units]))

    def tiles(body):
        @pl.loop(0, 3)
        def _(t):
            body(aligned(t * 256, 256, 256))

        body(pl.ds(768, 128))

    def product_of(lhs, rhs, transposed):
        def product(start, size, emit):
            at = aligned(start, size)

            def body(cols):
                if transposed:
                    v = lax.dot_general(
                        lhs[at, :], rhs[cols, :], (((1,), (1,)), ((), ())),
                        preferred_element_type=F32,
                    )
                else:
                    v = jnp.dot(lhs[at, :], rhs[:, cols], preferred_element_type=F32)
                emit(v, cols)
            tiles(body)
        return product

    gate_of = product_of(tok_all, w_gate, False)
    upper_of = product_of(tok_all, w_up, False)
    grad_of = product_of(cot_all, w_down, True)
    far, after, before = (x + 2) % 4, (x + 1) % 4, (x + 3) % 4

    def put(target, *terms):
        def emit(v, cols):
            for ref, at in terms:
                v = v + ref[at, cols].astype(F32)
            ref, at = target
            ref[at, cols] = v.astype(ref.dtype)
        return emit

    def reduce_x(product, s2, sp, sm, ia, ib, rp, rm, ys, yr, own):
        lo, hi, one = pl.ds(0, 256), pl.ds(256, 256), pl.ds(0, 256)
        product(far * 512, 256, put((s2, lo)))
        mid_a = send(s2.at[lo], ia, xp)
        product(far * 512 + 256, 256, put((s2, hi)))
        mid_b = send(s2.at[hi], ib, xm)
        yield
        product(after * 512 + 256, 256, put((sp, hi)))
        fin = [send(sp.at[hi], rp.at[hi], xp)]
        product(before * 512, 256, put((sm, lo)))
        fin.append(send(sm.at[lo], rm.at[lo], xm))
        yield
        mid_a.wait_recv()
        product(after * 512, 256, put((sp, lo), (ia, one)))
        fin.append(send(sp.at[lo], rp.at[lo], xp))
        mid_b.wait_recv()
        product(before * 512 + 256, 256, put((sm, hi), (ib, one)))
        fin.append(send(sm.at[hi], rm.at[hi], xm))
        yield
        for copy in fin:
            copy.wait_recv()

        def total(half, target):
            at = aligned(half * 256, 256, 256)
            product(x * 512 + half * 256, 256, put((target, one), (rp, at), (rm, at)))

        total(1 - h, ys)
        over = send(ys, yr, yh)
        total(h, own)
        yield
        over.wait_recv()
        yield

    def reduce_y(product, ys, yr, s2, sp, sm, ia, ib, rp, rm, own):
        chunks = (far, after, before, x)
        over = []
        lo, hi, one, two = pl.ds(0, 128), pl.ds(128, 128), pl.ds(0, 128), pl.ds(0, 256)

        def cross(k):
            at = pl.ds(k * 256, 256)
            product(chunks[k] * 512 + (1 - h) * 256, 256, put((ys, at)))
            over.append(send(ys.at[at], yr.at[at], yh))

        def mine(k, half):
            return chunks[k] * 512 + h * 256 + half * 128

        def came(k, half):
            return (yr, pl.ds(k * 256 + half * 128, 128))

        cross(0)
        yield
        for k in range(1, 4):
            cross(k)
        yield
        over[0].wait_recv()
        product(mine(0, 0), 256, put((s2, two), (yr, pl.ds(0, 256))))
        mid_a = send(s2.at[lo], ia, xp)
        mid_b = send(s2.at[hi], ib, xm)
        yield
        over[1].wait_recv()
        product(mine(1, 1), 128, put((sp, hi), came(1, 1)))
        fin = [send(sp.at[hi], rp.at[hi], xp)]
        yield
        over[2].wait_recv()
        product(mine(2, 0), 128, put((sm, lo), came(2, 0)))
        fin.append(send(sm.at[lo], rm.at[lo], xm))
        mid_a.wait_recv()
        product(mine(1, 0), 128, put((sp, lo), came(1, 0), (ia, one)))
        fin.append(send(sp.at[lo], rp.at[lo], xp))
        mid_b.wait_recv()
        product(mine(2, 1), 128, put((sm, hi), came(2, 1), (ib, one)))
        fin.append(send(sm.at[hi], rm.at[hi], xm))
        yield
        over[3].wait_recv()
        for copy in fin:
            copy.wait_recv()
        product(mine(3, 0), 256, put((own, two), (yr, pl.ds(768, 256)), (rp, two), (rm, two)))
        yield

    def spot_in(whole, x_, h_, part=0, size=256):
        return whole.at[aligned(x_ * 512 + h_ * 256 + part * 128, size)]

    def gather_y(own, whole, arrived=None):
        def came(x_, h_):
            if arrived is not None:
                arrived(x_, h_)

        spot = spot_in(whole, x, h)
        to_y = send(own, spot, yh)
        mine = local(own, spot)
        yield
        own_p, own_m = send(own, spot, xp), send(own, spot, xm)
        mine.wait()
        came(x, h)
        yield
        to_y.wait_recv()
        spot = spot_in(whole, x, 1 - h)
        mate_p, mate_m = send(spot, spot, xp), send(spot, spot, xm)
        came(x, 1 - h)
        yield
        halves = []
        for h_, from_m, from_p in ((h, own_p, own_m), (1 - h, mate_p, mate_m)):
            from_m.wait_recv()
            spot = spot_in(whole, before, h_, 0, 128)
            halves.append(send(spot, spot, xp))
            from_p.wait_recv()
            spot = spot_in(whole, after, h_, 1, 128)
            halves.append(send(spot, spot, xm))
            came(before, h_)
            came(after, h_)
            yield
        for i, h_ in enumerate((h, 1 - h)):
            halves[2 * i].wait_recv()
            halves[2 * i + 1].wait_recv()
            came(far, h_)
        yield

    def gather_x(own, whole):
        spot = spot_in(whole, x, h)
        own_p, own_m = send(own, spot, xp), send(own, spot, xm)
        mine = local(own, spot)
        yield
        over = [send(own, spot, yh)]
        yield
        own_p.wait_recv()
        spot = spot_in(whole, before, h, 0, 128)
        half_a = send(spot, spot, xp)
        spot = spot_in(whole, before, h)
        over.append(send(spot, spot, yh))
        own_m.wait_recv()
        spot = spot_in(whole, after, h, 1, 128)
        half_b = send(spot, spot, xm)
        spot = spot_in(whole, after, h)
        over.append(send(spot, spot, yh))
        yield
        half_a.wait_recv()
        half_b.wait_recv()
        spot = spot_in(whole, far, h)
        over.append(send(spot, spot, yh))
        yield
        for copy in over:
            copy.wait_recv()
        mine.wait()
        yield

    core = []

    def cross_core(x_, h_):
        pair = x_ * 2 + h_

        @pl.loop(0, 4)
        def _(t):
            cols = aligned(t * 256, 256, 256)
            c_s[pair, :, cols] = jnp.dot(
                hid_all[rows(pair * 2 + 1 - c), :], w_down[:, cols], preferred_element_type=F32
            )
        core.append(send(c_s.at[pair], c_r.at[pair], co))

    gate = reduce_x(gate_of, g_s2, g_sp, g_sm, g_ia, g_ib, g_rp, g_rm, g_ys, g_yr, g_own)
    upper = reduce_y(upper_of, u_ys, u_yr, u_s2, u_sp, u_sm, u_ia, u_ib, u_rp, u_rm, u_own)
    grad = reduce_x(grad_of, h_s2, h_sp, h_sm, h_ia, h_ib, h_rp, h_rm, h_ys, h_yr, h_own)
    next(gate)
    next(upper)
    next(gate)
    next(upper)
    next(cot_steps)
    flip(0, 2)
    next(cot_steps)
    next(upper)
    next(gate)
    next(upper)
    next(grad)
    next(grad)
    flip(2, 4)
    next(upper)
    flip(4, 6)
    next(gate)
    flip(6, 8)
    next(grad)
    next(upper)
    next(gate)

    @pl.loop(0, 16)
    def _(t):
        at = aligned(t * 16, 16, 16)
        gate_v = g_own[at, :] + g_yr[at, :].astype(F32)
        upper_v = u_own[at, :]
        sigma = 1.0 / (1.0 + jnp.exp(-gate_v))
        swish = gate_v * sigma
        hid_own[at, :] = (swish * upper_v).astype(BF)
        g_own[at, :] = upper_v * sigma * (1.0 + gate_v * (1.0 - sigma))
        u_own[at, :] = swish

    hid = gather_y(hid_own, hid_all, cross_core)
    next(hid)
    next(hid)
    next(grad)
    next(hid)
    next(hid)
    next(grad)

    @pl.loop(0, 16)
    def _(t):
        at = aligned(t * 16, 16, 16)
        grad_v = h_own[at, :] + h_yr[at, :].astype(F32)
        gp_own[at, :] = (grad_v * g_own[at, :]).astype(BF)
        up_own[at, :] = (grad_v * u_own[at, :]).astype(BF)

    gp = gather_x(gp_own, gp_hbm)
    up = gather_y(up_own, up_hbm)
    next(up)
    next(gp)
    next(gp)
    next(hid)
    next(up)
    next(hid)
    next(up)
    next(gp)

    def kept(yl_, z_):
        def piece(cols):
            part = jnp.dot(
                hid_all[rows(block(yl_, z_, c)), :], w_down[:, cols], preferred_element_type=F32
            )
            return part + c_r[yl_ * 4 + z_, :, cols]
        return piece

    def over_cols(body):
        @pl.loop(0, 4)
        def _(t):
            body(aligned(t * 256, 256, 256))

    down_grad(0)
    for copy in core:
        copy.wait_recv()
    z_far, z_after, z_before = (z + 2) % 4, (z + 1) % 4, (z + 3) % 4

    def ring_piece(y_, z_, target, inc=None):
        piece = kept(y_, z_)

        def body(cols):
            v = piece(cols)
            if inc is not None:
                v = v + inc[:, cols]
            target[:, cols] = v
        over_cols(body)

    ring_piece(0, z_far, z_s2.at[0])
    z_mid_a = send(z_s2.at[0], z_i.at[0], zp)
    ring_piece(1, z_far, z_s2.at[1])
    z_mid_b = send(z_s2.at[1], z_i.at[1], zm)
    ring_piece(1, z_after, z_sp.at[1])
    z_fin = [send(z_sp.at[1], z_rp.at[1], zp)]
    ring_piece(0, z_before, z_sm.at[0])
    z_fin.append(send(z_sm.at[0], z_rm.at[0], zm))
    next(up)
    next(gp)
    down_grad(1)
    down_grad(2)
    z_mid_a.wait_recv()
    ring_piece(0, z_after, z_sp.at[0], z_i.at[0])
    z_fin.append(send(z_sp.at[0], z_rp.at[0], zp))
    z_mid_b.wait_recv()
    ring_piece(1, z_before, z_sm.at[1], z_i.at[1])
    z_fin.append(send(z_sm.at[1], z_rm.at[1], zm))
    down_grad(3)
    down_grad(4)
    next(up)
    down_grad(5)
    down_grad(6)
    for copy in z_fin:
        copy.wait_recv()

    def row_total(y_, target):
        piece = kept(y_, z)

        def body(cols):
            total = piece(cols) + z_rp[y_, :, cols] + z_rm[y_, :, cols]
            target[:, cols] = total.astype(target.dtype)
        over_cols(body)

    row_total(1 - yl, o_ys)
    o_over = send(o_ys, o_yr, yn)
    row_total(yl, o_own)
    o_over.wait_recv()
    out[...] = (o_own[...] + o_yr[...].astype(F32)).astype(BF)
    next(up)
    next(gp)
    for copy in flips[-2:] + downs[-2:]:
        copy.wait()
    for copy in sent:
        copy.wait_send()


def forward(tokens, cotangent, gate_weight, up_weight, down_weight, keep_in, keep_out):
    hbm = pl.BlockSpec(memory_space=pl.ANY)
    vmem = pl.BlockSpec(memory_space=pltpu.VMEM)

    def bf(*shape):
        return pltpu.VMEM(shape, BF)

    def f32(*shape):
        return pltpu.VMEM(shape, F32)

    def ring(n):
        return [bf(n, 896)] * 3 + [bf(n // 2, 896)] * 2 + [bf(n, 896)] * 2

    def ring_y():
        return ring(512) + [bf(256, 896), bf(256, 896), f32(256, 896)]

    smem = pl.BlockSpec(memory_space=pltpu.SMEM)
    sds = jax.ShapeDtypeStruct
    return pl.pallas_call(
        forward_kernel,
        out_shape=(
            sds((128, 1024), BF), sds((1024, 2048), BF), sds((896, 1024), F32),
            sds((2048, 896), BF), sds((2048, 896), BF),
        ),
        in_specs=[vmem, vmem, hbm, hbm, hbm, smem, smem],
        out_specs=[vmem, hbm, hbm, hbm, hbm],
        scratch_shapes=[bf(1024, 896), bf(1024, 896), bf(896, 1024), bf(2048, 1024), bf(2048, 1024)]
        + ring_y()
        + ring_y()
        + [bf(1024, 896), bf(1024, 896)] + ring(256) + [f32(256, 896)]
        + [bf(256, 896)] * 3 + [bf(2048, 896)]
        + [f32(8, 128, 1024), f32(8, 128, 1024)]
        + [f32(2, 128, 1024)] * 6
        + [bf(128, 1024), bf(128, 1024), f32(128, 1024)]
        + [bf(2, 128, 2048), f32(2, 128, 1024)]
        + [
            pltpu.SemaphoreType.DMA((SLOTS,)), pltpu.SemaphoreType.DMA((SLOTS,)),
            pltpu.SemaphoreType.DMA((24,)),
        ],
        compiler_params=pltpu.CompilerParams(
            collective_id=0, has_side_effects=True, vmem_limit_bytes=VMEM_LIMIT
        ),
    )(tokens, cotangent, gate_weight, up_weight, down_weight, keep_in, keep_out)


def input_grads_kernel(
    keep_in, tok_t_hbm, gp_hbm, up_hbm, down_hbm, out_hbm,
    gate_grad, up_grad, down_grad, output, tok_t, gp, up, down, out, done, sems,
):
    lo, hi = slice(0, 512), slice(512, 1024)
    moves = (
        (tok_t_hbm.at[lo], tok_t.at[lo]), (gp_hbm, gp), (up_hbm, up),
        (tok_t_hbm.at[hi], tok_t.at[hi]), (down_hbm, down), (out_hbm, out),
    )
    loads = [pltpu.make_async_copy(src, dst, sems.at[i]) for i, (src, dst) in enumerate(moves)]
    for load in loads[:2]:
        load.start()
    stores = []

    def part(half, grads, target):
        k = len(stores)
        if k >= 2:
            stores[k - 2].wait()
        at = slice(half * 512, half * 512 + 512)
        buf = done.at[k % 2]

        def tile(start, first, blocks):
            for r in range(512 // K2_ROWS):
                some = slice(half * 512 + r * K2_ROWS, half * 512 + (r + 1) * K2_ROWS)
                v = jnp.dot(
                    tok_t[some, :], grads[:, aligned(start, blocks * 128)],
                    preferred_element_type=F32,
                )
                for i in range(K2_ROWS // 128):
                    for j in range(blocks):
                        kept_in = keep_in[(half * 512 + r * K2_ROWS) // 128 + i, first + j]
                        buf[
                            r * K2_ROWS + i * 128 : r * K2_ROWS + i * 128 + 128,
                            aligned(start + j * 128, 128),
                        ] = v[i * 128 : i * 128 + 128, j * 128 : j * 128 + 128] * kept_in.astype(F32)

        @pl.loop(0, 3)
        def _(t):
            tile(t * 256, 2 * t, 2)

        tile(768, 6, 1)
        store = pltpu.make_async_copy(buf, target.at[at], sems.at[6 + k])
        store.start()
        stores.append(store)

    loads[0].wait()
    loads[1].wait()
    for load in loads[2:4]:
        load.start()
    part(0, gp, gate_grad)
    loads[2].wait()
    loads[3].wait()
    for load in loads[4:]:
        load.start()
    part(0, up, up_grad)
    loads[4].wait()
    loads[5].wait()
    passed = [
        pltpu.make_async_copy(down, down_grad, sems.at[10]),
        pltpu.make_async_copy(out, output, sems.at[11]),
    ]
    for copy in passed:
        copy.start()
    part(1, gp, gate_grad)
    part(1, up, up_grad)
    for copy in passed + stores[2:]:
        copy.wait()


def input_grads(keep_in, tok_t, gp, up, down, out):
    hbm = pl.BlockSpec(memory_space=pl.ANY)
    sds = jax.ShapeDtypeStruct
    return pl.pallas_call(
        input_grads_kernel,
        out_shape=(
            sds((1024, 896), F32), sds((1024, 896), F32), sds((896, 1024), F32),
            sds((128, 1024), BF),
        ),
        in_specs=[pl.BlockSpec(memory_space=pltpu.SMEM)] + [hbm] * 5,
        out_specs=[hbm] * 4,
        scratch_shapes=[
            pltpu.VMEM((1024, 2048), BF), pltpu.VMEM((2048, 896), BF),
            pltpu.VMEM((2048, 896), BF), pltpu.VMEM((896, 1024), F32),
            pltpu.VMEM((128, 1024), BF), pltpu.VMEM((2, 512, 896), F32),
            pltpu.SemaphoreType.DMA((12,)),
        ],
        compiler_params=pltpu.CompilerParams(vmem_limit_bytes=VMEM_LIMIT),
    )(keep_in, tok_t, gp, up, down, out)


def shards(tokens, gate_weight, up_weight, down_weight, input_mask, output_mask, cotangent):
    out, tok_t, down, gp, up = forward(
        tokens, cotangent, gate_weight, up_weight, down_weight, input_mask, output_mask
    )
    grad_gate, grad_up, grad_down, output = input_grads(input_mask, tok_t, gp, up, down, out)
    return (output, grad_gate, grad_up, grad_down)


def solution(mesh):
    placed = (
        P("row", "col"), P("col", "row"), P("col", "row"), P("row", "col"),
        P("col", "row"), P("row", "col"), P("row", "col"),
    )
    return jax.shard_map(
        shards, mesh=mesh, in_specs=placed,
        out_specs=(P("row", "col"), P("col", "row"), P("col", "row"), P("row", "col")),
        check_vma=False,
    )
```

```python
import jax
import jax.numpy as jnp
from jax import lax
from jax.experimental import pallas as pl
from jax.experimental.pallas import tpu as pltpu
from jax.sharding import PartitionSpec as P

BF = jnp.bfloat16
F32 = jnp.float32
MESH = pl.DeviceIdType.MESH
VMEM_LIMIT = 62 * 2**20
SLOTS = 112
K2_ROWS = 256


def aligned(start, size, to=128):
    return pl.ds(pl.multiple_of(start, to), size)


def forward_kernel(
    tok, cot, gate_w, up_w, down_w, keep_in, keep_out,
    out, tok_t_hbm, down_hbm, gp_hbm, up_hbm,
    w_gate, w_up, w_down, tok_all, cot_all,
    g_s2, g_sp, g_sm, g_ia, g_ib, g_rp, g_rm, g_ys, g_yr, g_own,
    h_s2, h_sp, h_sm, h_ia, h_ib, h_rp, h_rm, h_ys, h_yr, h_own,
    u_ys, u_yr, u_s2, u_sp, u_sm, u_ia, u_ib, u_rp, u_rm, u_own,
    hid_own, gp_own, up_own, hid_all,
    c_s, c_r, z_s2, z_i, z_sp, z_sm, z_rp, z_rm, o_ys, o_yr, o_own, tok_t, down_t,
    send_sem, recv_sem, local_sem,
):
    row = lax.axis_index("row")
    col = lax.axis_index("col")
    x, h = col // 2, col % 2
    yl, z, c = row // 8, (row // 2) % 4, row % 2

    def device(x_, h_, yl_, z_, c_):
        return (yl_ * 8 + z_ * 2 + c_, x_ * 2 + h_)

    xp = device((x + 1) % 4, h, yl, z, c)
    xm = device((x + 3) % 4, h, yl, z, c)
    yh = device(x, 1 - h, yl, z, c)
    yn = device(x, h, 1 - yl, z, c)
    zp = device(x, h, yl, (z + 1) % 4, c)
    zm = device(x, h, yl, (z + 3) % 4, c)
    co = device(x, h, yl, z, 1 - c)
    peers = (xp, xm, yh, yn, zp, zm, co)

    slot = [0]
    sent = []

    def send(src, dst, peer):
        i = slot[0]
        slot[0] += 1
        copy = pltpu.make_async_remote_copy(
            src_ref=src, dst_ref=dst, send_sem=send_sem.at[i], recv_sem=recv_sem.at[i],
            device_id=peer, device_id_type=MESH,
        )
        copy.start()
        sent.append(copy)
        return copy

    locals_ = [0]

    def local(src, dst):
        copy = pltpu.make_async_copy(src, dst, local_sem.at[locals_[0]])
        locals_[0] += 1
        copy.start()
        return copy

    loads = [local(gate_w, w_gate), local(up_w, w_up), local(down_w, w_down)]

    barrier = pltpu.get_barrier_semaphore()
    for peer in peers:
        pl.semaphore_signal(barrier, inc=1, device_id=peer, device_id_type=MESH)
    pl.semaphore_wait(barrier, len(peers))

    def block(yl_, z_, c_):
        return yl_ * 8 + z_ * 2 + c_

    def rows(b, part=0, size=128):
        return aligned(b * 128 + part * 64, size, 64)

    def gather_row(own, whole):
        me = block(yl, z, c)
        spot = whole.at[rows(me)]
        to_y = send(own, spot, yn)
        own_p, own_m = send(own, spot, zp), send(own, spot, zm)
        cores = [send(own, spot, co)]
        whole[rows(me), :] = own[...]
        yield
        to_y.wait_recv()
        spot = whole.at[rows(block(1 - yl, z, c))]
        mate_p, mate_m = send(spot, spot, zp), send(spot, spot, zm)
        cores.append(send(spot, spot, co))
        halves = []
        for y_, from_m, from_p in ((yl, own_p, own_m), (1 - yl, mate_p, mate_m)):
            from_m.wait_recv()
            b = block(y_, (z + 3) % 4, c)
            spot = whole.at[rows(b, 0, 64)]
            first = send(spot, spot, zp)
            spot = whole.at[rows(b)]
            cores.append(send(spot, spot, co))
            from_p.wait_recv()
            b = block(y_, (z + 1) % 4, c)
            spot = whole.at[rows(b, 1, 64)]
            second = send(spot, spot, zm)
            spot = whole.at[rows(b)]
            cores.append(send(spot, spot, co))
            halves.append((y_, first, second))
        yield
        for y_, first, second in halves:
            first.wait_recv()
            second.wait_recv()
            spot = whole.at[rows(block(y_, (z + 2) % 4, c))]
            cores.append(send(spot, spot, co))
        for copy in cores:
            copy.wait_recv()
        yield

    tok_steps = gather_row(tok, tok_all)
    cot_steps = gather_row(cot, cot_all)
    next(tok_steps)

    for copy in loads:
        copy.wait()
    @pl.loop(0, 8)
    def _(i):
        at = aligned(i * 128, 128)
        for j in range(7):
            cols = slice(j * 128, j * 128 + 128)
            kept_in = keep_in[i, j].astype(F32)
            w_gate[at, cols] = (w_gate[at, cols].astype(F32) * kept_in).astype(BF)
            w_up[at, cols] = (w_up[at, cols].astype(F32) * kept_in).astype(BF)

    @pl.loop(0, 7)
    def _(i):
        at = aligned(i * 128, 128)
        for j in range(8):
            cols = slice(j * 128, j * 128 + 128)
            kept_out = keep_out[i, j].astype(F32)
            w_down[at, cols] = (w_down[at, cols].astype(F32) * kept_out).astype(BF)

    next(tok_steps)
    next(cot_steps)
    next(tok_steps)
    flips = []

    def flip(first, last):
        for i in range(first, last):
            if len(flips) >= 2:
                flips[-2].wait()
            at = slice(i * 128, i * 128 + 128)
            tok_t[i % 2] = tok_all[:, at].T
            flips.append(local(tok_t.at[i % 2], tok_t_hbm.at[at]))

    downs = []

    def down_grad(i):
        if len(downs) >= 2:
            downs[-2].wait()
        units = slice(i * 128, i * 128 + 128)
        left = hid_all[:, units].T

        @pl.loop(0, 4)
        def _(t):
            v = jnp.dot(left, cot_all[:, aligned(t * 256, 256, 256)], preferred_element_type=F32)
            for j in range(2):
                kept_out = keep_out[i, 2 * t + j].astype(F32)
                down_t[i % 2, :, aligned(t * 256 + j * 128, 128)] = (
                    v[:, j * 128 : j * 128 + 128] * kept_out
                )
        downs.append(local(down_t.at[i % 2], down_hbm.at[units]))

    def tiles(body):
        @pl.loop(0, 3)
        def _(t):
            body(aligned(t * 256, 256, 256))

        body(pl.ds(768, 128))

    def product_of(lhs, rhs, transposed):
        def product(start, size, emit):
            at = aligned(start, size)

            def body(cols):
                if transposed:
                    v = lax.dot_general(
                        lhs[at, :], rhs[cols, :], (((1,), (1,)), ((), ())),
                        preferred_element_type=F32,
                    )
                else:
                    v = jnp.dot(lhs[at, :], rhs[:, cols], preferred_element_type=F32)
                emit(v, cols)
            tiles(body)
        return product

    gate_of = product_of(tok_all, w_gate, False)
    upper_of = product_of(tok_all, w_up, False)
    grad_of = product_of(cot_all, w_down, True)
    far, after, before = (x + 2) % 4, (x + 1) % 4, (x + 3) % 4

    def put(target, *terms):
        def emit(v, cols):
            for ref, at in terms:
                v = v + ref[at, cols].astype(F32)
            ref, at = target
            ref[at, cols] = v.astype(ref.dtype)
        return emit

    def reduce_x(product, s2, sp, sm, ia, ib, rp, rm, ys, yr, own):
        lo, hi, one = pl.ds(0, 256), pl.ds(256, 256), pl.ds(0, 256)
        product(far * 512, 256, put((s2, lo)))
        mid_a = send(s2.at[lo], ia, xp)
        product(far * 512 + 256, 256, put((s2, hi)))
        mid_b = send(s2.at[hi], ib, xm)
        yield
        product(after * 512 + 256, 256, put((sp, hi)))
        fin = [send(sp.at[hi], rp.at[hi], xp)]
        product(before * 512, 256, put((sm, lo)))
        fin.append(send(sm.at[lo], rm.at[lo], xm))
        yield
        mid_a.wait_recv()
        product(after * 512, 256, put((sp, lo), (ia, one)))
        fin.append(send(sp.at[lo], rp.at[lo], xp))
        mid_b.wait_recv()
        product(before * 512 + 256, 256, put((sm, hi), (ib, one)))
        fin.append(send(sm.at[hi], rm.at[hi], xm))
        yield
        for copy in fin:
            copy.wait_recv()

        def total(half, target):
            at = aligned(half * 256, 256, 256)
            product(x * 512 + half * 256, 256, put((target, one), (rp, at), (rm, at)))

        total(1 - h, ys)
        over = send(ys, yr, yh)
        total(h, own)
        yield
        over.wait_recv()
        yield

    def reduce_y(product, ys, yr, s2, sp, sm, ia, ib, rp, rm, own):
        chunks = (far, after, before, x)
        over = []
        lo, hi, one, two = pl.ds(0, 128), pl.ds(128, 128), pl.ds(0, 128), pl.ds(0, 256)

        def cross(k):
            at = pl.ds(k * 256, 256)
            product(chunks[k] * 512 + (1 - h) * 256, 256, put((ys, at)))
            over.append(send(ys.at[at], yr.at[at], yh))

        def mine(k, half):
            return chunks[k] * 512 + h * 256 + half * 128

        def came(k, half):
            return (yr, pl.ds(k * 256 + half * 128, 128))

        cross(0)
        yield
        for k in range(1, 4):
            cross(k)
        yield
        over[0].wait_recv()
        product(mine(0, 0), 256, put((s2, two), (yr, pl.ds(0, 256))))
        mid_a = send(s2.at[lo], ia, xp)
        mid_b = send(s2.at[hi], ib, xm)
        yield
        over[1].wait_recv()
        product(mine(1, 1), 128, put((sp, hi), came(1, 1)))
        fin = [send(sp.at[hi], rp.at[hi], xp)]
        yield
        over[2].wait_recv()
        product(mine(2, 0), 128, put((sm, lo), came(2, 0)))
        fin.append(send(sm.at[lo], rm.at[lo], xm))
        mid_a.wait_recv()
        product(mine(1, 0), 128, put((sp, lo), came(1, 0), (ia, one)))
        fin.append(send(sp.at[lo], rp.at[lo], xp))
        mid_b.wait_recv()
        product(mine(2, 1), 128, put((sm, hi), came(2, 1), (ib, one)))
        fin.append(send(sm.at[hi], rm.at[hi], xm))
        yield
        over[3].wait_recv()
        for copy in fin:
            copy.wait_recv()
        product(mine(3, 0), 256, put((own, two), (yr, pl.ds(768, 256)), (rp, two), (rm, two)))
        yield

    def spot_in(whole, x_, h_, part=0, size=256):
        return whole.at[aligned(x_ * 512 + h_ * 256 + part * 128, size)]

    def gather_y(own, whole, arrived=None):
        def came(x_, h_):
            if arrived is not None:
                arrived(x_, h_)

        spot = spot_in(whole, x, h)
        to_y = send(own, spot, yh)
        mine = local(own, spot)
        yield
        own_p, own_m = send(own, spot, xp), send(own, spot, xm)
        mine.wait()
        came(x, h)
        yield
        to_y.wait_recv()
        spot = spot_in(whole, x, 1 - h)
        mate_p, mate_m = send(spot, spot, xp), send(spot, spot, xm)
        came(x, 1 - h)
        yield
        halves = []
        for h_, from_m, from_p in ((h, own_p, own_m), (1 - h, mate_p, mate_m)):
            from_m.wait_recv()
            spot = spot_in(whole, before, h_, 0, 128)
            halves.append(send(spot, spot, xp))
            from_p.wait_recv()
            spot = spot_in(whole, after, h_, 1, 128)
            halves.append(send(spot, spot, xm))
            came(before, h_)
            came(after, h_)
            yield
        for i, h_ in enumerate((h, 1 - h)):
            halves[2 * i].wait_recv()
            halves[2 * i + 1].wait_recv()
            came(far, h_)
        yield

    def gather_x(own, whole):
        spot = spot_in(whole, x, h)
        own_p, own_m = send(own, spot, xp), send(own, spot, xm)
        mine = local(own, spot)
        yield
        over = [send(own, spot, yh)]
        yield
        own_p.wait_recv()
        spot = spot_in(whole, before, h, 0, 128)
        half_a = send(spot, spot, xp)
        spot = spot_in(whole, before, h)
        over.append(send(spot, spot, yh))
        own_m.wait_recv()
        spot = spot_in(whole, after, h, 1, 128)
        half_b = send(spot, spot, xm)
        spot = spot_in(whole, after, h)
        over.append(send(spot, spot, yh))
        yield
        half_a.wait_recv()
        half_b.wait_recv()
        spot = spot_in(whole, far, h)
        over.append(send(spot, spot, yh))
        yield
        for copy in over:
            copy.wait_recv()
        mine.wait()
        yield

    core = []

    def cross_core(x_, h_):
        pair = x_ * 2 + h_

        @pl.loop(0, 4)
        def _(t):
            cols = aligned(t * 256, 256, 256)
            c_s[pair, :, cols] = jnp.dot(
                hid_all[rows(pair * 2 + 1 - c), :], w_down[:, cols], preferred_element_type=F32
            )
        core.append(send(c_s.at[pair], c_r.at[pair], co))

    gate = reduce_x(gate_of, g_s2, g_sp, g_sm, g_ia, g_ib, g_rp, g_rm, g_ys, g_yr, g_own)
    upper = reduce_y(upper_of, u_ys, u_yr, u_s2, u_sp, u_sm, u_ia, u_ib, u_rp, u_rm, u_own)
    grad = reduce_x(grad_of, h_s2, h_sp, h_sm, h_ia, h_ib, h_rp, h_rm, h_ys, h_yr, h_own)
    next(gate)
    next(upper)
    next(gate)
    next(upper)
    next(cot_steps)
    flip(0, 2)
    next(cot_steps)
    next(upper)
    next(gate)
    next(upper)
    next(grad)
    next(grad)
    flip(2, 4)
    next(upper)
    flip(4, 6)
    next(gate)
    flip(6, 8)
    next(grad)
    next(upper)
    next(gate)

    @pl.loop(0, 16)
    def _(t):
        at = aligned(t * 16, 16, 16)
        gate_v = g_own[at, :] + g_yr[at, :].astype(F32)
        upper_v = u_own[at, :]
        sigma = 1.0 / (1.0 + jnp.exp(-gate_v))
        swish = gate_v * sigma
        hid_own[at, :] = (swish * upper_v).astype(BF)
        g_own[at, :] = upper_v * sigma * (1.0 + gate_v * (1.0 - sigma))
        u_own[at, :] = swish

    hid = gather_y(hid_own, hid_all, cross_core)
    next(hid)
    next(hid)
    next(grad)
    next(hid)
    next(hid)
    next(grad)

    @pl.loop(0, 16)
    def _(t):
        at = aligned(t * 16, 16, 16)
        grad_v = h_own[at, :] + h_yr[at, :].astype(F32)
        gp_own[at, :] = (grad_v * g_own[at, :]).astype(BF)
        up_own[at, :] = (grad_v * u_own[at, :]).astype(BF)

    gp = gather_x(gp_own, gp_hbm)
    up = gather_y(up_own, up_hbm)
    next(up)
    next(gp)
    next(gp)
    next(hid)
    next(up)
    next(hid)
    next(up)
    next(gp)

    def kept(yl_, z_):
        def piece(cols):
            part = jnp.dot(
                hid_all[rows(block(yl_, z_, c)), :], w_down[:, cols], preferred_element_type=F32
            )
            return part + c_r[yl_ * 4 + z_, :, cols]
        return piece

    def over_cols(body):
        @pl.loop(0, 4)
        def _(t):
            body(aligned(t * 256, 256, 256))

    down_grad(0)
    for copy in core:
        copy.wait_recv()
    z_far, z_after, z_before = (z + 2) % 4, (z + 1) % 4, (z + 3) % 4

    def ring_piece(y_, z_, target, inc=None):
        piece = kept(y_, z_)

        def body(cols):
            v = piece(cols)
            if inc is not None:
                v = v + inc[:, cols]
            target[:, cols] = v
        over_cols(body)

    ring_piece(0, z_far, z_s2.at[0])
    z_mid_a = send(z_s2.at[0], z_i.at[0], zp)
    ring_piece(1, z_far, z_s2.at[1])
    z_mid_b = send(z_s2.at[1], z_i.at[1], zm)
    ring_piece(1, z_after, z_sp.at[1])
    z_fin = [send(z_sp.at[1], z_rp.at[1], zp)]
    ring_piece(0, z_before, z_sm.at[0])
    z_fin.append(send(z_sm.at[0], z_rm.at[0], zm))
    next(up)
    next(gp)
    down_grad(1)
    down_grad(2)
    z_mid_a.wait_recv()
    ring_piece(0, z_after, z_sp.at[0], z_i.at[0])
    z_fin.append(send(z_sp.at[0], z_rp.at[0], zp))
    z_mid_b.wait_recv()
    ring_piece(1, z_before, z_sm.at[1], z_i.at[1])
    z_fin.append(send(z_sm.at[1], z_rm.at[1], zm))
    down_grad(3)
    down_grad(4)
    next(up)
    for copy in z_fin:
        copy.wait_recv()

    def row_total(y_, target):
        piece = kept(y_, z)

        def body(cols):
            total = piece(cols) + z_rp[y_, :, cols] + z_rm[y_, :, cols]
            target[:, cols] = total.astype(target.dtype)
        over_cols(body)

    row_total(1 - yl, o_ys)
    o_over = send(o_ys, o_yr, yn)
    row_total(yl, o_own)
    down_grad(5)
    down_grad(6)
    o_over.wait_recv()
    out[...] = (o_own[...] + o_yr[...].astype(F32)).astype(BF)
    next(up)
    next(gp)
    for copy in flips[-2:] + downs[-2:]:
        copy.wait()
    for copy in sent:
        copy.wait_send()


def forward(tokens, cotangent, gate_weight, up_weight, down_weight, keep_in, keep_out):
    hbm = pl.BlockSpec(memory_space=pl.ANY)
    vmem = pl.BlockSpec(memory_space=pltpu.VMEM)

    def bf(*shape):
        return pltpu.VMEM(shape, BF)

    def f32(*shape):
        return pltpu.VMEM(shape, F32)

    def ring(n):
        return [bf(n, 896)] * 3 + [bf(n // 2, 896)] * 2 + [bf(n, 896)] * 2

    def ring_y():
        return ring(512) + [bf(256, 896), bf(256, 896), f32(256, 896)]

    smem = pl.BlockSpec(memory_space=pltpu.SMEM)
    sds = jax.ShapeDtypeStruct
    return pl.pallas_call(
        forward_kernel,
        out_shape=(
            sds((128, 1024), BF), sds((1024, 2048), BF), sds((896, 1024), F32),
            sds((2048, 896), BF), sds((2048, 896), BF),
        ),
        in_specs=[vmem, vmem, hbm, hbm, hbm, smem, smem],
        out_specs=[vmem, hbm, hbm, hbm, hbm],
        scratch_shapes=[bf(1024, 896), bf(1024, 896), bf(896, 1024), bf(2048, 1024), bf(2048, 1024)]
        + ring_y()
        + ring_y()
        + [bf(1024, 896), bf(1024, 896)] + ring(256) + [f32(256, 896)]
        + [bf(256, 896)] * 3 + [bf(2048, 896)]
        + [f32(8, 128, 1024), f32(8, 128, 1024)]
        + [f32(2, 128, 1024)] * 6
        + [bf(128, 1024), bf(128, 1024), f32(128, 1024)]
        + [bf(2, 128, 2048), f32(2, 128, 1024)]
        + [
            pltpu.SemaphoreType.DMA((SLOTS,)), pltpu.SemaphoreType.DMA((SLOTS,)),
            pltpu.SemaphoreType.DMA((24,)),
        ],
        compiler_params=pltpu.CompilerParams(
            collective_id=0, has_side_effects=True, vmem_limit_bytes=VMEM_LIMIT
        ),
    )(tokens, cotangent, gate_weight, up_weight, down_weight, keep_in, keep_out)


def input_grads_kernel(
    keep_in, tok_t_hbm, gp_hbm, up_hbm, down_hbm, out_hbm,
    gate_grad, up_grad, down_grad, output, tok_t, gp, up, down, out, done, sems,
):
    lo, hi = slice(0, 512), slice(512, 1024)
    moves = (
        (tok_t_hbm.at[lo], tok_t.at[lo]), (gp_hbm, gp), (up_hbm, up),
        (tok_t_hbm.at[hi], tok_t.at[hi]), (down_hbm, down), (out_hbm, out),
    )
    loads = [pltpu.make_async_copy(src, dst, sems.at[i]) for i, (src, dst) in enumerate(moves)]
    for load in loads[:2]:
        load.start()
    stores = []

    def part(half, grads, target):
        k = len(stores)
        if k >= 2:
            stores[k - 2].wait()
        at = slice(half * 512, half * 512 + 512)
        buf = done.at[k % 2]

        def tile(start, first, blocks):
            for r in range(512 // K2_ROWS):
                some = slice(half * 512 + r * K2_ROWS, half * 512 + (r + 1) * K2_ROWS)
                v = jnp.dot(
                    tok_t[some, :], grads[:, aligned(start, blocks * 128)],
                    preferred_element_type=F32,
                )
                for i in range(K2_ROWS // 128):
                    for j in range(blocks):
                        kept_in = keep_in[(half * 512 + r * K2_ROWS) // 128 + i, first + j]
                        buf[
                            r * K2_ROWS + i * 128 : r * K2_ROWS + i * 128 + 128,
                            aligned(start + j * 128, 128),
                        ] = v[i * 128 : i * 128 + 128, j * 128 : j * 128 + 128] * kept_in.astype(F32)

        @pl.loop(0, 3)
        def _(t):
            tile(t * 256, 2 * t, 2)

        tile(768, 6, 1)
        store = pltpu.make_async_copy(buf, target.at[at], sems.at[6 + k])
        store.start()
        stores.append(store)

    loads[0].wait()
    loads[1].wait()
    for load in loads[2:4]:
        load.start()
    part(0, gp, gate_grad)
    loads[2].wait()
    loads[3].wait()
    for load in loads[4:]:
        load.start()
    part(0, up, up_grad)
    loads[4].wait()
    loads[5].wait()
    passed = [
        pltpu.make_async_copy(down, down_grad, sems.at[10]),
        pltpu.make_async_copy(out, output, sems.at[11]),
    ]
    for copy in passed:
        copy.start()
    part(1, gp, gate_grad)
    part(1, up, up_grad)
    for copy in passed + stores[2:]:
        copy.wait()


def input_grads(keep_in, tok_t, gp, up, down, out):
    hbm = pl.BlockSpec(memory_space=pl.ANY)
    sds = jax.ShapeDtypeStruct
    return pl.pallas_call(
        input_grads_kernel,
        out_shape=(
            sds((1024, 896), F32), sds((1024, 896), F32), sds((896, 1024), F32),
            sds((128, 1024), BF),
        ),
        in_specs=[pl.BlockSpec(memory_space=pltpu.SMEM)] + [hbm] * 5,
        out_specs=[hbm] * 4,
        scratch_shapes=[
            pltpu.VMEM((1024, 2048), BF), pltpu.VMEM((2048, 896), BF),
            pltpu.VMEM((2048, 896), BF), pltpu.VMEM((896, 1024), F32),
            pltpu.VMEM((128, 1024), BF), pltpu.VMEM((2, 512, 896), F32),
            pltpu.SemaphoreType.DMA((12,)),
        ],
        compiler_params=pltpu.CompilerParams(vmem_limit_bytes=VMEM_LIMIT),
    )(keep_in, tok_t, gp, up, down, out)


def shards(tokens, gate_weight, up_weight, down_weight, input_mask, output_mask, cotangent):
    out, tok_t, down, gp, up = forward(
        tokens, cotangent, gate_weight, up_weight, down_weight, input_mask, output_mask
    )
    grad_gate, grad_up, grad_down, output = input_grads(input_mask, tok_t, gp, up, down, out)
    return (output, grad_gate, grad_up, grad_down)


def solution(mesh):
    placed = (
        P("row", "col"), P("col", "row"), P("col", "row"), P("row", "col"),
        P("col", "row"), P("row", "col"), P("row", "col"),
    )
    return jax.shard_map(
        shards, mesh=mesh, in_specs=placed,
        out_specs=(P("row", "col"), P("col", "row"), P("col", "row"), P("row", "col")),
        check_vma=False,
    )
```
